512 devices in a mesh: blocks: 128 (over z, x, core), vol: 4 (over y).
Axes of the slice: x: 4, y: 4, z: 16, core: 2. Of those that a mesh axis runs over, the one named last changes fastest.
Arguments:
- features: bfloat16 [4, 1024, 16384], P('vol', 'blocks'), may hold values from -6 to 6
- active: int32 [4, 1024], P('vol', 'blocks'), may hold values 0 or 1
- coarse_grad: bfloat16 [4, 128, 32768], P('vol', 'blocks'), may hold values from -6 to 6
- conv_weight: bfloat16 [27, 32, 32], replicated, may hold values from -0.21875 to 0.21875
- down_weight: bfloat16 [8, 32, 64], replicated, may hold values from -0.375 to 0.375
Outputs:
- feature_grad: bfloat16 [4, 1024, 16384], P('vol', 'blocks')
- conv_weight_grad: float32 [27, 32, 32], replicated
- down_weight_grad: float32 [8, 32, 64], replicated
The draws below stay inside these ranges and needn't reach their ends.
All inputs are finite; a program needn't handle non-finite values. No bound on the sum of `active` on one device may be relied on, other than what follows from the above.
Results may differ from the reference program's by a relative error of at most 0.0065.
Values may be sent and summed in bfloat16 or wider, within the bound.
No kernel may reach another device: no remote copies, remote signals or barrier semaphores. Data moves between devices by JAX's collectives and lax.ppermute only.
A program may use at most 128 MiB of HBM per device.

```python
import jax
import jax.numpy as jnp
from jax import lax

C1 = 32
C2 = 64
EDGE = 8
SIDE = 2
LAYERS = 2
VOX = 512
BLOCKS = 1024
CBLOCKS = 128
SLABS = 4
N_BLOCKS = 128


def place_ends(array, rng, least, largest):
    longest = array.shape.index(max(array.shape))
    spots = []
    for shift in (0, 1):
        where = [jax.random.randint(jax.random.fold_in(rng, axis), (), 0, length) for axis, length in enumerate(array.shape)]
        where[longest] = (where[longest] + shift) % array.shape[longest]
        spots.append(tuple(where))
    return array.at[spots[0]].set(least).at[spots[1]].set(largest)


def levels(key, extent, split, low, high):
    loudness = 1.0
    for dim, blocks in split:
        heights = jax.random.uniform(jax.random.fold_in(jax.random.fold_in(key, 6), dim), (blocks,), jnp.float32, low / len(split), high / len(split))
        loudness = loudness * jnp.repeat(jnp.exp(heights), extent[dim] // blocks).reshape((-1,) + (1,) * (len(extent) - 1 - dim))
    return loudness


def gaussian(own_key, extent, spread, reach, shards=(), kind=jnp.bfloat16):
    level = levels(own_key, extent, shards, -0.22, 0.18) if shards else 1.0
    values = jax.random.normal(own_key, extent, jnp.float32) * spread * level
    return jnp.minimum(jnp.maximum(values, -reach), reach).astype(kind)


def setup_inputs(seed: int = 0) -> dict:
    key_list = jax.random.split(jax.random.key(seed), 6)
    return {
        "features": gaussian(key_list[0], (SLABS, BLOCKS, VOX * C1), 1.0, 6.0, ((0, 4), (1, 128))),
        "active": place_ends((jax.random.randint(key_list[1], (SLABS, BLOCKS), 0, 4) < 3).astype(jnp.int32), jax.random.fold_in(key_list[1], 1), 0, 1),
        "coarse_grad": gaussian(key_list[2], (SLABS, CBLOCKS, VOX * C2), 1.0, 6.0, ((0, 4), (1, 128))),
        "conv_weight": gaussian(key_list[3], (27, C1, C1), (27 * C1) ** -0.5, 0.21875),
        "down_weight": gaussian(key_list[4], (8, C1, C2), (8 * C1) ** -0.5, 0.375),
    }


def to_grid(tiles, layers, side, edge, chans):
    cube = tiles.reshape(layers, side, side, edge, edge, edge, chans)
    return cube.transpose(0, 3, 1, 4, 2, 5, 6).reshape(layers * edge, side * edge, side * edge, chans)

def to_tiles(grid, layers, side, edge, chans):
    cube = grid.reshape(layers, edge, side, edge, side, edge, chans)
    return cube.transpose(0, 2, 4, 1, 3, 5, 6).reshape(layers * side * side, edge ** 3 * chans)

def convolve(volume, kernel):
    return lax.conv_general_dilated(volume[None], kernel, (1, 1, 1), ((1, 1), (1, 1), (1, 1)), dimension_numbers=('NDHWC', 'DHWIO', 'NDHWC'), precision=lax.Precision.HIGHEST)[0]

def reference(features, active, coarse_grad, conv_weight, down_weight):
    total_layers = LAYERS * N_BLOCKS
    scale = 1.0 / jnp.sqrt(jnp.float32(SLABS * BLOCKS * VOX))
    kernel = conv_weight.astype(jnp.float32).reshape(3, 3, 3, C1, C1)
    flipped = kernel[::-1, ::-1, ::-1].transpose(0, 1, 2, 4, 3)
    down = down_weight.astype(jnp.float32).reshape(2, 2, 2, C1, C2)
    conv_total = jnp.zeros((27, C1, C1), jnp.float32)
    down_total = jnp.zeros((8, C1, C2), jnp.float32)
    grads = []
    for slab in range(SLABS):
        depth = total_layers * EDGE
        width = SIDE * EDGE
        mask = jnp.broadcast_to(active[slab].reshape(total_layers, 1, SIDE, 1, SIDE, 1, 1).astype(jnp.float32), (total_layers, EDGE, SIDE, EDGE, SIDE, EDGE, 1)).reshape(depth, width, width, 1)
        grid = to_grid(features[slab], total_layers, SIDE, EDGE, C1)
        masked = (grid.astype(jnp.float32) * mask).astype(jnp.bfloat16)
        pre = convolve(masked.astype(jnp.float32), kernel)
        sig = jax.nn.sigmoid(pre)
        ystate = (masked.astype(jnp.float32) + mask * pre * sig).astype(jnp.bfloat16)
        coarse = to_grid(coarse_grad[slab], total_layers // 2, SIDE // 2, EDGE, C2).astype(jnp.float32)
        dy = jnp.einsum('abcn,pqrmn->apbqcrm', coarse, down, precision=lax.Precision.HIGHEST).reshape(depth, width, width, C1)
        ysix = ystate.astype(jnp.float32).reshape(depth // 2, 2, width // 2, 2, width // 2, 2, C1)
        down_total = down_total + jnp.einsum('apbqcrm,abcn->pqrmn', ysix, coarse, precision=lax.Precision.HIGHEST).reshape(8, C1, C2)
        dpre = (mask * dy * sig * (1.0 + pre * (1.0 - sig))).astype(jnp.bfloat16)
        back = convolve(dpre.astype(jnp.float32), flipped)
        grads.append(to_tiles((mask * (dy + back)).astype(jnp.bfloat16), total_layers, SIDE, EDGE, C1))
        padded = jnp.pad(masked.astype(jnp.float32), ((1, 1), (1, 1), (1, 1), (0, 0)))
        dflat = dpre.astype(jnp.float32).reshape(-1, C1)
        terms = []
        for index in range(27):
            oz, oy, ox = (index // 9, index // 3 % 3, index % 3)
            window = padded[oz:oz + depth, oy:oy + width, ox:ox + width].reshape(-1, C1)
            terms.append(jnp.dot(window.T, dflat, precision=lax.Precision.HIGHEST))
        conv_total = conv_total + jnp.stack(terms)
    return (jnp.stack(grads), conv_total * scale, down_total * scale)
```

```python
import jax
import jax.numpy as jnp
from jax import lax
from jax.sharding import Mesh
from jax.sharding import PartitionSpec as P

BLOCKS = ("z", "x", "core")
EDGE = 8
SIDE = 2


def extended(block, sides, width):
    for axis, dim in sides:
        count = lax.axis_size(axis)
        forward = [(i, i + 1) for i in range(count - 1)]
        backward = [(target, source) for source, target in forward]
        low = lax.ppermute(
            lax.slice_in_dim(block, block.shape[dim] - width, None, axis=dim), axis, forward
        )
        high = lax.ppermute(lax.slice_in_dim(block, 0, width, axis=dim), axis, backward)
        block = jnp.concatenate([low, block, high], axis=dim)
    return block


def to_grid(tiles, layers, side, edge, chans):
    cube = tiles.reshape(layers, side, side, edge, edge, edge, chans)
    return cube.transpose(0, 3, 1, 4, 2, 5, 6).reshape(
        layers * edge, side * edge, side * edge * chans
    )


def to_tiles(grid, layers, side, edge, chans):
    cube = grid.reshape(layers, edge, side, edge, side, edge, chans)
    return cube.transpose(0, 2, 4, 1, 3, 5, 6).reshape(layers * side * side, edge**3 * chans)


def shifters(width):
    rows = jnp.arange(width)[None, :, None]
    cols = jnp.arange(width)[None, None, :]
    offset = jnp.arange(3)[:, None, None]
    return (rows == cols + offset - 1).astype(jnp.float32)


def banded(kernel, width, chans):
    matrix = jnp.einsum("oij,zyoab->zyiajb", shifters(width), kernel.astype(jnp.float32))
    return matrix.reshape(3, 3, width * chans, width * chans).astype(jnp.bfloat16)


def forward_conv(volume, matrix, depth, width):
    padded = jnp.pad(volume, ((0, 0), (1, 1), (0, 0)))
    total = None
    for index in range(9):
        oz, oy = (index // 3, index % 3)
        term = lax.dot_general(
            padded[oz : oz + depth, oy : oy + width],
            matrix[oz, oy],
            (((2,), (0,)), ((), ())),
            preferred_element_type=jnp.float32,
        )
        total = term if total is None else total + term
    return total


def backward_conv(volume, matrix, depth, width):
    padded = jnp.pad(volume, ((0, 0), (1, 1), (0, 0)))
    total = None
    for index in range(9):
        oz, oy = (index // 3, index % 3)
        term = lax.dot_general(
            padded[2 - oz : 2 - oz + depth, 2 - oy : 2 - oy + width],
            matrix[oz, oy],
            (((2,), (1,)), ((), ())),
            preferred_element_type=jnp.float32,
        )
        total = term if total is None else total + term
    return total


def kernel_grad(volume, dpre, depth, width, chans):
    padded = jnp.pad(volume, ((0, 0), (1, 1), (0, 0)))
    shift_table = shifters(width)
    terms = []
    for index in range(9):
        oz, oy = (index // 3, index % 3)
        outer = lax.dot_general(
            padded[oz : oz + depth, oy : oy + width],
            dpre,
            (((0, 1), (0, 1)), ((), ())),
            preferred_element_type=jnp.float32,
        )
        terms.append(
            jnp.einsum("oij,iajb->oab", shift_table, outer.reshape(width, chans, width, chans))
        )
    return jnp.stack(terms).reshape(27, chans, chans)


def shards(features, active, coarse_grad, conv_weight, down_weight):
    slots = features.shape[1]
    chans = conv_weight.shape[1]
    outs = down_weight.shape[2]
    layers = slots // (SIDE * SIDE)
    depth = layers * EDGE
    width = SIDE * EDGE
    scale = 1.0 / jnp.sqrt(
        jnp.float32(lax.axis_size("vol") * lax.axis_size(BLOCKS) * slots * EDGE**3)
    )
    live = active[0].astype(jnp.bfloat16)
    masked = features[0] * live[:, None]
    mask = jnp.broadcast_to(
        active[0].reshape(layers, 1, SIDE, 1, SIDE, 1, 1).astype(jnp.float32),
        (layers, EDGE, SIDE, EDGE, SIDE, EDGE, chans),
    ).reshape(depth, width, width * chans)
    matrix = banded(conv_weight.reshape(3, 3, 3, chans, chans), width, chans)
    coarse = to_grid(coarse_grad[0], layers // 2, SIDE // 2, EDGE, outs).reshape(
        depth // 2, width // 2, width // 2, outs
    )
    down = down_weight.reshape(2, 2, 2, chans, outs)
    wide = extended(masked, ((BLOCKS, 0),), SIDE * SIDE)
    deep = to_grid(wide, layers + 2, SIDE, EDGE, chans)[EDGE - 1 : EDGE + depth + 1]
    grid = deep[1:-1]
    pre = forward_conv(deep, matrix, depth, width)
    sig = jax.nn.sigmoid(pre)
    ystate = (grid.astype(jnp.float32) + mask * pre * sig).astype(jnp.bfloat16)
    dy = jnp.einsum(
        "abcn,pqrmn->apbqcrm", coarse, down, preferred_element_type=jnp.float32
    ).reshape(depth, width, width * chans)
    ysix = ystate.reshape(depth // 2, 2, width // 2, 2, width // 2, 2, chans)
    down_part = jnp.einsum(
        "apbqcrm,abcn->pqrmn", ysix, coarse, preferred_element_type=jnp.float32
    ).reshape(8, chans, outs)
    dpre = (mask * dy * sig * (1.0 + pre * (1.0 - sig))).astype(jnp.bfloat16)
    dpre_tiles = to_tiles(dpre, layers, SIDE, EDGE, chans)
    dpre_wide = extended(dpre_tiles, ((BLOCKS, 0),), SIDE * SIDE)
    dpre_deep = to_grid(dpre_wide, layers + 2, SIDE, EDGE, chans)[EDGE - 1 : EDGE + depth + 1]
    back = backward_conv(dpre_deep, matrix, depth, width)
    result = to_tiles((mask * (dy + back)).astype(jnp.bfloat16), layers, SIDE, EDGE, chans)
    conv_part = kernel_grad(deep, dpre, depth, width, chans)
    conv_total, down_total = total((conv_part, down_part))
    return (result[None], conv_total * scale, down_total * scale)


def total(parts):
    sizes = [part.size for part in parts]
    near = ("x", "core", "vol")
    count = lax.axis_size(near)
    flat = jnp.concatenate([part.reshape(-1) for part in parts])
    piece = -(-flat.size // (count * 128)) * 128
    flat = jnp.pad(flat, (0, piece * count - flat.size))
    cut = flat.reshape(count, piece // 128, 128)
    mine = lax.all_to_all(cut, near, 0, 0).sum(0)
    far = lax.axis_size("z")
    mine = lax.all_to_all(jnp.broadcast_to(mine[None], (far,) + mine.shape), "z", 0, 0).sum(0)
    whole = lax.all_to_all(jnp.broadcast_to(mine[None], (count,) + mine.shape), near, 0, 0)
    whole = whole.reshape(-1)
    outs, start = [], 0
    for part, size in zip(parts, sizes):
        outs.append(whole[start : start + size].reshape(part.shape))
        start += size
    return outs


def solution(mesh):
    fine = Mesh(
        mesh.devices.reshape(-1, 4, 2, mesh.shape["vol"]), BLOCKS + ("vol",)
    )
    placed = (P("vol", BLOCKS, None), P("vol", BLOCKS), P("vol", BLOCKS, None), P(), P())
    return jax.shard_map(
        shards,
        mesh=fine,
        in_specs=placed,
        out_specs=(P("vol", BLOCKS, None), P(), P()),
        check_vma=False,
    )
```

```python
import jax
import jax.numpy as jnp
from jax import lax
from jax.experimental import pallas as pl
from jax.experimental.pallas import tpu as pltpu
from jax.sharding import Mesh
from jax.sharding import PartitionSpec as P

BLOCKS = ("z", "x", "core")
NEAR = ("x", "core", "vol")
F32 = jnp.float32
BF16 = jnp.bfloat16

ROW = 256
WIDE = 384
PIECE = 16


def iota(shape, dim):
    return lax.broadcasted_iota(jnp.int32, shape, dim)


def live_rows(active_ref, lanes):
    slot = iota((8, lanes), 0)
    out = jnp.zeros((8, lanes), F32)
    for b in range(8):
        out = jnp.where(slot == b, active_ref[0, b].astype(F32), out)
    return out


def repeat_lanes(rows, lanes):
    return (iota((rows, lanes), 1) % rows == iota((rows, lanes), 0)).astype(BF16)


def widen(row):
    slot, lane = iota((8, 128), 0), iota((8, 128), 1)
    right = pltpu.roll(row[:, :128], 7, 0)
    left = pltpu.roll(row[:, 128:], 1, 0)
    edge = jnp.where(
        (slot % 2 == 0) & (lane < 32), right, jnp.where((slot % 2 == 1) & (lane >= 96), left, 0.0)
    )
    return jnp.concatenate([row, edge], axis=1)


def put_plane(outer, inner, z, rows):
    full = [widen(row) for row in rows]
    upper = (iota((8, WIDE), 0) // 2) % 2
    low = jnp.where(upper == 1, pltpu.roll(full[7], 2, 0), 0.0)
    high = jnp.where(upper == 0, pltpu.roll(full[0], 6, 0), 0.0)
    ring = [low] + full + [high]
    for k in range(5):
        outer[z, 16 * k : 16 * k + 16] = jnp.concatenate(ring[2 * k : 2 * k + 2], 0).astype(BF16)
    for k in range(4):
        inner[z, 16 * k : 16 * k + 16] = jnp.concatenate(full[2 * k : 2 * k + 2], 0).astype(BF16)


def window(outer, inner, first, count, oz, oy):
    source = inner if oy == 1 else outer
    start = 16 if oy == 2 else 0
    return source[first + oz : first + oz + count, start : start + 64, :].reshape(count * 64, WIDE)


def put_bands(bands, index, taps):
    spot = iota((32, ROW), 1) // 32
    for i in range(8):
        part = jnp.zeros((32, ROW), F32)
        for ox in range(3):
            part = jnp.where(spot == i + 1 - ox, taps[ox], part)
        bands[index, 32 * i : 32 * i + 32] = part.astype(BF16)
    bands[index, 256:288] = jnp.where(spot == 7, taps[2], 0.0).astype(BF16)
    bands[index, 288:352] = jnp.zeros((64, ROW), BF16)
    bands[index, 352:384] = jnp.where(spot == 0, taps[0], 0.0).astype(BF16)


def pack_kernel(active, features, coarse, to_next, to_prev, coarse_rows):
    live = live_rows(active, ROW)
    slot = iota((8, ROW), 0)
    row, col = iota((128, 128), 0), iota((128, 128), 1)
    zc, yc, b = row // 32, (row // 8) % 4, row % 8
    source = (((b // 4) * 4 + zc) * 8 + ((b // 2) % 2) * 4 + yc) * 2 + b % 2
    kept = jnp.concatenate([live[:, :128]] * 16, axis=0)
    pick = jnp.where(source == col, kept, 0.0).astype(BF16)
    rows = jnp.dot(pick, coarse[...], preferred_element_type=F32)
    coarse_rows[...] = rows.astype(BF16)

    def fine(z, y):
        start = (z * 8 + y) * ROW
        return features[:, start : start + ROW].astype(F32) * live

    for y in range(8):
        lanes = slice(y * ROW, y * ROW + ROW)
        to_next[:, lanes] = jnp.where(slot < 4, pltpu.roll(fine(6, y), 4, 0), fine(7, y)).astype(BF16)
        to_prev[:, lanes] = jnp.where(slot < 4, fine(1, y), pltpu.roll(fine(0, y), 4, 0)).astype(BF16)
    for k in range(2):
        lanes = slice(2048 + k * ROW, 2048 + k * ROW + ROW)
        last = [rows[96 + 8 * y : 104 + 8 * y] for y in (2 * k, 2 * k + 1)]
        first = [rows[8 * y : 8 * y + 8] for y in (2 * k, 2 * k + 1)]
        to_next[:, lanes] = jnp.where(slot < 4, pltpu.roll(last[0], 4, 0), last[1]).astype(BF16)
        to_prev[:, lanes] = jnp.where(slot < 4, first[1], pltpu.roll(first[0], 4, 0)).astype(BF16)


def inner_kernel(active, features, conv, down, outer, inner, bands, spread):
    live = live_rows(active, ROW)
    for z in range(8):
        rows = []
        for y in range(8):
            start = (z * 8 + y) * ROW
            rows.append(features[:, start : start + ROW].astype(F32) * live)
        put_plane(outer, inner, z, rows)
    tile = repeat_lanes(32, ROW)
    taps = jnp.dot(conv[...].reshape(27 * 32, 32), tile, preferred_element_type=F32)
    for index in range(9):
        put_bands(bands, index, [taps[96 * index + 32 * ox : 96 * index + 32 * ox + 32] for ox in range(3)])
    spot = iota((64, ROW), 1) // 32
    for q in range(4):
        turned = [
            lax.dot_general(down[2 * q + ox], tile, (((0,), (0,)), ((), ())), preferred_element_type=F32)
            for ox in range(2)
        ]
        for cx in range(4):
            part = jnp.where(spot == 2 * cx, turned[0], jnp.where(spot == 2 * cx + 1, turned[1], 0.0))
            spread[64 * cx : 64 * cx + 64, ROW * q : ROW * q + ROW] = part.astype(BF16)


def main_kernel(
    scale, inner_own, outer_own, from_prev, from_next, coarse_rows, bands, spread,
    grads, dpre, dy, outer, inner, coarse, pre, spread_out, state,
):
    slot = iota((8, ROW), 0)
    outer[2:10] = outer_own[...]
    inner[2:10] = inner_own[...]

    def own(z, y):
        return inner_own[z, 16 * (y // 2) : 16 * (y // 2) + 16, :ROW].astype(F32)[8 * (y % 2) : 8 * (y % 2) + 8]

    before, beyond, after, past = [], [], [], []
    for y in range(8):
        low = from_prev[:, y * ROW : y * ROW + ROW].astype(F32)
        high = from_next[:, y * ROW : y * ROW + ROW].astype(F32)
        beyond.append(jnp.where(slot < 4, low, pltpu.roll(own(6, y), 4, 0)))
        before.append(pltpu.roll(jnp.where(slot >= 4, low, own(7, y)), 4, 0))
        after.append(jnp.where(slot >= 4, high, pltpu.roll(own(0, y), 4, 0)))
        past.append(pltpu.roll(jnp.where(slot < 4, high, own(1, y)), 4, 0))
    for z, rows in ((0, beyond), (1, before), (10, after), (11, past)):
        put_plane(outer, inner, z, rows)

    coarse[32:160] = coarse_rows[...]
    for k in range(2):
        lanes = slice(2048 + k * ROW, 2048 + k * ROW + ROW)
        low, high = from_prev[:, lanes].astype(F32), from_next[:, lanes].astype(F32)
        last = coarse_rows[96 + 16 * k : 112 + 16 * k].astype(F32)
        first = coarse_rows[16 * k : 16 * k + 16].astype(F32)
        under = [
            jnp.where(slot < 4, low, pltpu.roll(last[:8], 4, 0)),
            pltpu.roll(jnp.where(slot >= 4, low, last[8:]), 4, 0),
        ]
        over = [
            jnp.where(slot >= 4, high, pltpu.roll(first[:8], 4, 0)),
            pltpu.roll(jnp.where(slot < 4, high, first[8:]), 4, 0),
        ]
        coarse[16 * k : 16 * k + 16] = jnp.concatenate(under, 0).astype(BF16)
        coarse[160 + 16 * k : 176 + 16 * k] = jnp.concatenate(over, 0).astype(BF16)

    spread_out[...] = jnp.dot(coarse[...], spread[...], preferred_element_type=F32)
    total = None
    for oz in range(3):
        for oy in range(3):
            term = jnp.dot(
                window(outer, inner, 0, 10, oz, oy), bands[3 * oz + oy], preferred_element_type=F32
            )
            total = term if total is None else total + term
    pre[...] = total

    for step in range(10):
        z = step - 1
        zc, qz = z // 2 + 1, z % 2
        slope = []
        for pair in range(4):
            rows = slice(64 * step + 16 * pair, 64 * step + 16 * pair + 16)
            u = pre[rows]
            sig = 0.5 * jnp.tanh(0.5 * u) + 0.5
            silu = u * sig
            base = 32 * zc + 8 * pair
            back = jnp.concatenate(
                [spread_out[base : base + 8, ROW * (2 * qz + qy) : ROW * (2 * qz + qy) + ROW] for qy in range(2)], 0
            )
            dpre[step, 16 * pair : 16 * pair + 16] = (back * sig * (1.0 + (u - silu))).astype(BF16)
            if 0 <= z < 8:
                dy[z, 16 * pair : 16 * pair + 16] = back
                slope.append(inner[z + 2, 16 * pair : 16 * pair + 16, :ROW].astype(F32) + silu)
        if 0 <= z < 8:
            for qy in range(2):
                for half in range(2):
                    y = jnp.concatenate(
                        [slope[2 * half + k][8 * qy : 8 * qy + 8] for k in range(2)], 0
                    )
                    start = 32 * (z // 2) + 16 * half
                    state[2 * qz + qy, start : start + 16] = y.astype(BF16)

    lane = iota((32, 128), 1)
    turned = dpre[1:9].reshape(512, ROW).astype(F32).T.astype(BF16)
    for index in range(9):
        outer_sum = jnp.dot(
            turned, window(outer, inner, 1, 8, index // 3, index % 3), preferred_element_type=F32
        )
        block = [outer_sum[32 * j : 32 * j + 32] for j in range(8)]
        v0, v1, edge = slice(0, 128), slice(128, 256), slice(256, 384)
        t0 = jnp.where(lane >= 96, block[0][:, edge] + block[4][:, v0], block[0][:, v0] + block[4][:, v1])
        t1 = block[1][:, v0] + block[5][:, v1]
        t2 = block[2][:, v0] + block[6][:, v1]
        t3 = jnp.where(lane < 32, block[3][:, v1] + block[7][:, edge], block[3][:, v0] + block[7][:, v1])
        folded = pltpu.roll(t0, 32, 1) + t1 + pltpu.roll(t2, 96, 1) + pltpu.roll(t3, 64, 1)
        grads[32 * index : 32 * index + 32] = jnp.where(lane < 96, folded * scale, 0.0)
    own_coarse = coarse[32:160]
    for q in range(4):
        outer_sum = lax.dot_general(
            state[q], own_coarse, (((0,), (0,)), ((), ())), preferred_element_type=F32
        )
        block = [outer_sum[32 * x : 32 * x + 32] for x in range(8)]
        even = [block[qx][:, :128] + block[4 + qx][:, 128:] for qx in range(2)]
        odd = [block[2 + qx][:, :128] + block[6 + qx][:, 128:] for qx in range(2)]
        folded = jnp.where(lane < 64, even[0], odd[1]) + pltpu.roll(
            jnp.where(lane < 64, even[1], odd[0]), 64, 1
        )
        grads[288 + 32 * q : 320 + 32 * q] = folded * scale
    grads[416:512] = jnp.zeros((96, 128), F32)


def back_kernel(active, conv, dpre, dy, result, outer, inner, bands):
    live = live_rows(active, ROW)
    tile = repeat_lanes(32, ROW)
    for index in range(9):
        taps = [
            lax.dot_general(
                conv[26 - (3 * index + ox)], tile, (((0,), (0,)), ((), ())), preferred_element_type=F32
            )
            for ox in range(3)
        ]
        put_bands(bands, index, taps)
    for z in range(10):
        rows = []
        for pair in range(4):
            both = dpre[z, 16 * pair : 16 * pair + 16].astype(F32)
            rows += [both[:8], both[8:]]
        put_plane(outer, inner, z, rows)
    total = None
    for oz in range(3):
        for oy in range(3):
            term = jnp.dot(
                window(outer, inner, 0, 8, oz, oy), bands[3 * oz + oy], preferred_element_type=F32
            )
            total = term if total is None else total + term
    for z in range(8):
        for y in range(8):
            row = 64 * z + 8 * y
            value = dy[z, 8 * y : 8 * y + 8] + live * total[row : row + 8]
            result[:, row * 32 : row * 32 + ROW] = value.astype(BF16)


def sum_kernel(parts, out):
    total = parts[0]
    for k in range(1, parts.shape[0]):
        total = total + parts[k]
    for k in range(out.shape[0]):
        out[k] = total.astype(out.dtype)


def finish_kernel(whole, conv_grad, down_grad):
    def rows(start, count):
        parts = []
        for piece in range(start // PIECE, (start + count) // PIECE):
            parts.append(whole[piece].astype(F32))
        return jnp.concatenate(parts, 0)

    for index in range(9):
        turned = rows(32 * index, 32).T
        for ox in range(3):
            conv_grad[3 * index + ox] = turned[32 * ox : 32 * ox + 32]
    for q in range(4):
        both = rows(288 + 32 * q, 32)
        down_grad[2 * q] = both[:, :64]
        down_grad[2 * q + 1] = pltpu.roll(both, 64, 1)[:, :64]


def call(kernel, outs, scalars, arrays, scratch=(), name=None):
    spaces = [pltpu.SMEM] * len(scalars) + [pltpu.VMEM] * len(arrays)
    return pl.pallas_call(
        kernel,
        out_shape=[jax.ShapeDtypeStruct(shape, dtype) for shape, dtype in outs],
        in_specs=[pl.BlockSpec(memory_space=space) for space in spaces],
        out_specs=[pl.BlockSpec(memory_space=pltpu.VMEM)] * len(outs),
        scratch_shapes=[pltpu.VMEM(shape, dtype) for shape, dtype in scratch],
        compiler_params=pltpu.CompilerParams(vmem_limit_bytes=40 * 2**20),
        name=name,
    )(*scalars, *arrays)


def shards(features, active, coarse_grad, conv_weight, down_weight):
    fine = features[0]
    devices = lax.axis_size(BLOCKS)
    scale = (lax.axis_size("vol") * devices * fine.size // 32) ** -0.5
    to_next, to_prev, coarse_rows = call(
        pack_kernel,
        [((8, 2560), BF16), ((8, 2560), BF16), ((128, ROW), BF16)],
        [active], [fine, coarse_grad.reshape(128, ROW)], name="pack",
    )
    up = [(i, i + 1) for i in range(devices - 1)]
    from_prev = lax.ppermute(to_next, BLOCKS, up)
    from_next = lax.ppermute(to_prev, BLOCKS, [(j, i) for i, j in up])
    outer, inner, bands, spread = call(
        inner_kernel,
        [((8, 80, WIDE), BF16), ((8, 64, WIDE), BF16), ((9, WIDE, ROW), BF16), ((ROW, 4 * ROW), BF16)],
        [active], [fine, conv_weight, down_weight], name="inner",
    )
    grads, dpre, dy = call(
        lambda *refs: main_kernel(scale, *refs),
        [((512, 128), F32), ((10, 64, ROW), BF16), ((8, 64, ROW), F32)],
        [], [inner, outer, from_prev, from_next, coarse_rows, bands, spread],
        [
            ((12, 80, WIDE), BF16), ((12, 64, WIDE), BF16), ((192, ROW), BF16),
            ((640, ROW), F32), ((192, 4 * ROW), F32), ((4, 128, ROW), BF16),
        ],
        name="main",
    )
    count, far = lax.axis_size(NEAR), lax.axis_size("z")
    pieces = 512 // PIECE
    cut = grads.reshape(count, pieces // count, PIECE, 128) if count != pieces else grads.reshape(count, PIECE, 128)
    cut = lax.all_to_all(cut, NEAR, 0, 0)
    (result,) = call(
        back_kernel, [((8, 64 * ROW), BF16)],
        [active], [conv_weight, dpre, dy],
        [((10, 80, WIDE), BF16), ((10, 64, WIDE), BF16), ((9, WIDE, ROW), BF16)],
        name="back",
    )
    (mine,) = call(sum_kernel, [((far,) + cut.shape[1:], F32)], [], [cut], name="sum_near")
    mine = lax.all_to_all(mine, "z", 0, 0)
    (mine,) = call(sum_kernel, [(cut.shape, F32)], [], [mine], name="sum_far")
    whole = lax.all_to_all(mine, NEAR, 0, 0).reshape(pieces, PIECE, 128)
    conv_grad, down_grad = call(
        finish_kernel, [((27, 32, 32), F32), ((8, 32, 64), F32)], [], [whole], name="finish"
    )
    return result[None], conv_grad, down_grad


def solution(mesh):
    fine = Mesh(mesh.devices.reshape(-1, 4, 2, mesh.shape["vol"]), BLOCKS + ("vol",))
    placed = (P("vol", BLOCKS, None), P("vol", BLOCKS), P("vol", BLOCKS, None), P(), P())
    return jax.shard_map(
        shards,
        mesh=fine,
        in_specs=placed,
        out_specs=(P("vol", BLOCKS, None), P(), P()),
        check_vma=False,
    )
```

```python
import jax
import jax.numpy as jnp
from jax import lax
from jax.experimental import pallas as pl
from jax.experimental.pallas import tpu as pltpu
from jax.sharding import Mesh
from jax.sharding import PartitionSpec as P

BLOCKS = ("z", "x", "core")
NEAR = ("x", "core", "vol")
F32 = jnp.float32
BF16 = jnp.bfloat16

ROW = 256
WIDE = 384
PIECE = 16


def iota(shape, dim):
    return lax.broadcasted_iota(jnp.int32, shape, dim)


def live_rows(active_ref):
    slot = iota((8, ROW), 0)
    out = jnp.zeros((8, ROW), F32)
    for b in range(8):
        out = jnp.where(slot == b, active_ref[0, b].astype(F32), out)
    return out


def repeat_lanes(rows, lanes):
    return (iota((rows, lanes), 1) % rows == iota((rows, lanes), 0)).astype(BF16)


def widen(row, halves):
    slot, lane = iota((8, 128), 0), iota((8, 128), 1)
    first, second = row[:, :128], row[:, 128:]
    right = pltpu.roll(first, 7, 0)
    left = pltpu.roll(second, 1, 0)
    edge = jnp.where(
        (slot % 2 == 0) & (lane < 32), right, jnp.where((slot % 2 == 1) & (lane >= 96), left, 0.0)
    )
    parts = [first, second, edge]
    if halves:
        parts += [jnp.where(lane >= 96, edge, second), jnp.where(lane < 32, edge, first)]
    return jnp.concatenate(parts, axis=1)


def put_plane(outer, inner, z, rows, halves=True):
    full = [widen(row, halves) for row in rows]
    upper = (iota(full[0].shape, 0) // 2) % 2
    low = jnp.where(upper == 1, pltpu.roll(full[7], 2, 0), 0.0)
    high = jnp.where(upper == 0, pltpu.roll(full[0], 6, 0), 0.0)
    ring = [low] + full + [high]
    for k in range(5):
        outer[z, 16 * k : 16 * k + 16] = jnp.concatenate(ring[2 * k : 2 * k + 2], 0).astype(BF16)
    for k in range(4):
        inner[z, 16 * k : 16 * k + 16] = jnp.concatenate(full[2 * k : 2 * k + 2], 0).astype(BF16)


def window(outer, inner, first, count, oz, oy, lanes):
    source = inner if oy == 1 else outer
    start = 16 if oy == 2 else 0
    rows = source[first + oz : first + oz + count, start : start + 64, lanes]
    return rows.reshape(count * 64, rows.shape[-1])


def convolve(outer, inner, bands, first, count):
    left = [
        window(outer, inner, first, count, index // 3, index % 3, slice(0, WIDE)) for index in range(9)
    ]
    return jnp.dot(
        jnp.concatenate(left, 1), bands[...].reshape(9 * WIDE, ROW), preferred_element_type=F32
    )


def slopes(pre, dy, fine):
    sig = 0.5 * jnp.tanh(0.5 * pre) + 0.5
    silu = pre * sig
    return (dy * sig * (1.0 + (pre - silu))).astype(BF16), fine + silu


def put_state(state, z, rows):
    for qy in range(2):
        for half in range(2):
            pair = [rows[2 * half + k][8 * qy : 8 * qy + 8] for k in range(2)]
            start = 32 * (z // 2) + 16 * half
            state[2 * (z % 2) + qy, start : start + 16] = jnp.concatenate(pair, 0).astype(BF16)


def put_bands(bands, index, taps):
    spot = iota((32, ROW), 1) // 32
    for i in range(8):
        part = jnp.zeros((32, ROW), F32)
        for ox in range(3):
            part = jnp.where(spot == i + 1 - ox, taps[ox], part)
        bands[index, 32 * i : 32 * i + 32] = part.astype(BF16)
    bands[index, 256:288] = jnp.where(spot == 7, taps[2], 0.0).astype(BF16)
    bands[index, 288:352] = jnp.zeros((64, ROW), BF16)
    bands[index, 352:384] = jnp.where(spot == 0, taps[0], 0.0).astype(BF16)


def pack_kernel(
    active, features, coarse, conv, down, to_next, to_prev, coarse_rows, live_out, fine_out, conv_out, down_out,
    flags, flat, sems,
):
    ends = [slice(0, 4096), slice(12288, 16384), slice(4096, 12288)]
    copies = [
        pltpu.make_async_copy(active, flags, sems.at[0]),
        pltpu.make_async_copy(coarse, flat, sems.at[1]),
    ]
    copies += [
        pltpu.make_async_copy(features.at[:, lanes], fine_out.at[:, lanes], sems.at[2 + k])
        for k, lanes in enumerate(ends)
    ]
    copies += [
        pltpu.make_async_copy(conv, conv_out, sems.at[5]),
        pltpu.make_async_copy(down, down_out, sems.at[6]),
    ]
    for copy in copies:
        copy.start()
    copies[0].wait()
    live = live_rows(flags)
    live_out[...] = live
    slot = iota((8, ROW), 0)
    copies[1].wait()

    def coarse_row(zc, yc):
        parts = []
        for b in range(8):
            start = ((((b // 4) * 4 + zc) * 8 + ((b // 2) % 2) * 4 + yc) * 2 + b % 2) * ROW
            parts.append(flat[:, start : start + ROW].astype(F32))
        return jnp.concatenate(parts, 0) * live

    ends = {}
    for zc in range(4):
        for half in range(2):
            both = [coarse_row(zc, 2 * half + k) for k in range(2)]
            start = 32 * zc + 16 * half
            coarse_rows[start : start + 16] = jnp.concatenate(both, 0).astype(BF16)
            ends[zc, half] = both
    for half in range(2):
        lanes = slice(2048 + half * ROW, 2048 + half * ROW + ROW)
        last, first = ends[3, half], ends[0, half]
        to_next[:, lanes] = jnp.where(slot < 4, pltpu.roll(last[0], 4, 0), last[1]).astype(BF16)
        to_prev[:, lanes] = jnp.where(slot < 4, first[1], pltpu.roll(first[0], 4, 0)).astype(BF16)

    def fine(z, y):
        start = (z * 8 + y) * ROW
        return fine_out[:, start : start + ROW].astype(F32) * live

    copies[2].wait()
    copies[3].wait()
    for y in range(8):
        lanes = slice(y * ROW, y * ROW + ROW)
        to_next[:, lanes] = jnp.where(slot < 4, pltpu.roll(fine(6, y), 4, 0), fine(7, y)).astype(BF16)
        to_prev[:, lanes] = jnp.where(slot < 4, fine(1, y), pltpu.roll(fine(0, y), 4, 0)).astype(BF16)
    for copy in copies[4:]:
        copy.wait()


def inner_kernel(
    live_in, features, conv, down, coarse, outer, inner, bands, spread, dpre, dy, state, pre, spread_out,
):
    live = live_in[...]
    tile = repeat_lanes(32, ROW)
    spot = iota((64, ROW), 1) // 32
    for q in range(4):
        turned = [
            lax.dot_general(down[2 * q + ox], tile, (((0,), (0,)), ((), ())), preferred_element_type=F32)
            for ox in range(2)
        ]
        for cx in range(4):
            part = jnp.where(spot == 2 * cx, turned[0], jnp.where(spot == 2 * cx + 1, turned[1], 0.0))
            spread[64 * cx : 64 * cx + 64, ROW * q : ROW * q + ROW] = part.astype(BF16)
    spread_out[...] = jnp.dot(coarse[...], spread[...], preferred_element_type=F32)
    taps = jnp.dot(conv[...].reshape(27 * 32, 32), tile, preferred_element_type=F32)
    for index in range(9):
        put_bands(bands, index, [taps[96 * index + 32 * ox : 96 * index + 32 * ox + 32] for ox in range(3)])
    for z in range(8):
        rows = []
        for y in range(8):
            start = (z * 8 + y) * ROW
            rows.append(features[:, start : start + ROW].astype(F32) * live)
        put_plane(outer, inner, z, rows)
    pre[...] = convolve(outer, inner, bands, 0, 6)
    for z in range(8):
        qz, rows = z % 2, []
        for pair in range(4):
            part = slice(16 * pair, 16 * pair + 16)
            base = 32 * (z // 2) + 8 * pair
            lanes = [slice(ROW * (2 * qz + qy), ROW * (2 * qz + qy) + ROW) for qy in range(2)]
            spread_rows = jnp.concatenate([spread_out[base : base + 8, lane] for lane in lanes], 0)
            dy[z, part] = spread_rows
            if 1 <= z <= 6:
                start = 64 * (z - 1) + 16 * pair
                fine = inner[z, part, :ROW].astype(F32)
                dpre[z - 1, part], y = slopes(pre[start : start + 16], spread_rows, fine)
                rows.append(y)
        if rows:
            put_state(state, z, rows)
    for z in (0, 7):
        put_state(state, z, [jnp.zeros((16, ROW), F32)] * 4)


def main_kernel(
    scale, inner_own, outer_own, from_prev, from_next, coarse, bands, spread, dpre_own, dy, state_own,
    grads, dpre, outer, inner, ends, pre, state,
):
    slot = iota((8, ROW), 0)
    outer[2:10] = outer_own[...]
    inner[2:10] = inner_own[...]
    dpre[2:8] = dpre_own[...]
    state[...] = state_own[...]

    def own(z, y):
        return inner_own[z, 16 * (y // 2) : 16 * (y // 2) + 16, :ROW].astype(F32)[8 * (y % 2) : 8 * (y % 2) + 8]

    before, beyond, after, past = [], [], [], []
    for y in range(8):
        low = from_prev[:, y * ROW : y * ROW + ROW].astype(F32)
        high = from_next[:, y * ROW : y * ROW + ROW].astype(F32)
        beyond.append(jnp.where(slot < 4, low, pltpu.roll(own(6, y), 4, 0)))
        before.append(pltpu.roll(jnp.where(slot >= 4, low, own(7, y)), 4, 0))
        after.append(jnp.where(slot >= 4, high, pltpu.roll(own(0, y), 4, 0)))
        past.append(pltpu.roll(jnp.where(slot < 4, high, own(1, y)), 4, 0))
    for z, rows in ((0, beyond), (1, before), (10, after), (11, past)):
        put_plane(outer, inner, z, rows)

    for k in range(2):
        lanes = slice(2048 + k * ROW, 2048 + k * ROW + ROW)
        low, high = from_prev[:, lanes].astype(F32), from_next[:, lanes].astype(F32)
        last = coarse[96 + 16 * k : 112 + 16 * k].astype(F32)
        first = coarse[16 * k : 16 * k + 16].astype(F32)
        under = [
            jnp.where(slot < 4, low, pltpu.roll(last[:8], 4, 0)),
            pltpu.roll(jnp.where(slot >= 4, low, last[8:]), 4, 0),
        ]
        over = [
            jnp.where(slot >= 4, high, pltpu.roll(first[:8], 4, 0)),
            pltpu.roll(jnp.where(slot < 4, high, first[8:]), 4, 0),
        ]
        ends[0, 16 * k : 16 * k + 16] = jnp.concatenate(under, 0).astype(BF16)
        ends[1, 16 * k : 16 * k + 16] = jnp.concatenate(over, 0).astype(BF16)
    dy_end = [
        jnp.dot(ends[0], spread[:, 2 * ROW :], preferred_element_type=F32),
        jnp.dot(ends[1], spread[:, : 2 * ROW], preferred_element_type=F32),
    ]

    for side in range(2):
        pre[side] = convolve(outer, inner, bands, 8 * side, 2)
    for side in range(2):
        for k in range(2):
            step = 8 * side + k
            z = step - 1
            rows = []
            for pair in range(4):
                part = slice(16 * pair, 16 * pair + 16)
                if 0 <= z < 8:
                    back = dy[z, part]
                else:
                    back = jnp.concatenate(
                        [dy_end[side][8 * pair : 8 * pair + 8, ROW * qy : ROW * qy + ROW] for qy in range(2)], 0
                    )
                start = 64 * k + 16 * pair
                fine = inner[step + 1, part, :ROW].astype(F32)
                dpre[step, part], y = slopes(pre[side, start : start + 16], back, fine)
                rows.append(y)
            if 0 <= z < 8:
                put_state(state, z, rows)

    lane = iota((32, 128), 1)
    v0, v1, low1, high1 = slice(0, 128), slice(128, 256), slice(384, 512), slice(512, 640)
    turned = dpre[1:9].reshape(512, ROW).T
    turned = jnp.concatenate([turned[:128], turned[128:]], 1)
    for oz in range(3):
        right = []
        for oy in range(3):
            halves = [
                jnp.concatenate([window(outer, inner, 1, 8, oz, oy, part) for part in parts], 1)
                for parts in ((v0, low1), (v1, high1))
            ]
            right.append(jnp.concatenate(halves, 0))
        products = jnp.dot(turned, jnp.concatenate(right, 1), preferred_element_type=F32)
        for oy in range(3):
            block = [products[32 * j : 32 * j + 32, ROW * oy : ROW * oy + ROW] for j in range(4)]
            t0 = jnp.where(lane >= 96, block[0][:, v1], block[0][:, v0])
            t3 = jnp.where(lane < 32, block[3][:, v1], block[3][:, v0])
            folded = (
                pltpu.roll(t0, 32, 1)
                + block[1][:, v0]
                + pltpu.roll(block[2][:, v0], 96, 1)
                + pltpu.roll(t3, 64, 1)
            )
            start = 32 * (3 * oz + oy)
            grads[start : start + 32] = jnp.where(lane < 96, folded * scale, 0.0)
    left = jnp.concatenate(
        [jnp.concatenate([state[q][:, v0], state[q][:, v1]], 0) for q in range(4)], 1
    )
    right = jnp.concatenate([coarse[:, v0], coarse[:, v1]], 0)
    products = lax.dot_general(left, right, (((0,), (0,)), ((), ())), preferred_element_type=F32)
    for q in range(4):
        block = [products[128 * q + 32 * x : 128 * q + 32 * x + 32] for x in range(4)]
        folded = jnp.where(lane < 64, block[0], block[3]) + pltpu.roll(
            jnp.where(lane < 64, block[1], block[2]), 64, 1
        )
        grads[288 + 32 * q : 320 + 32 * q] = folded * scale
    grads[416:512] = jnp.zeros((96, 128), F32)


def back_kernel(live_in, conv, dpre, dy, result, outer, inner, bands):
    live = live_in[...]
    tile = repeat_lanes(32, ROW)
    for index in range(9):
        taps = [
            lax.dot_general(
                conv[26 - (3 * index + ox)], tile, (((0,), (0,)), ((), ())), preferred_element_type=F32
            )
            for ox in range(3)
        ]
        put_bands(bands, index, taps)
    for z in range(10):
        rows = []
        for pair in range(4):
            both = dpre[z, 16 * pair : 16 * pair + 16].astype(F32)
            rows += [both[:8], both[8:]]
        put_plane(outer, inner, z, rows, halves=False)
    total = convolve(outer, inner, bands, 0, 8)
    for z in range(8):
        for y in range(8):
            row = 64 * z + 8 * y
            value = dy[z, 8 * y : 8 * y + 8] + live * total[row : row + 8]
            result[:, row * 32 : row * 32 + ROW] = value.astype(BF16)


def sum_kernel(parts, out):
    total = parts[0]
    for k in range(1, parts.shape[0]):
        total = total + parts[k]
    for k in range(out.shape[0]):
        out[k] = total.astype(out.dtype)


def finish_kernel(whole, conv_grad, down_grad):
    def rows(start, count):
        parts = []
        for piece in range(start // PIECE, (start + count) // PIECE):
            parts.append(whole[piece].astype(F32))
        return jnp.concatenate(parts, 0)

    for index in range(9):
        turned = rows(32 * index, 32).T
        for ox in range(3):
            conv_grad[3 * index + ox] = turned[32 * ox : 32 * ox + 32]
    for q in range(4):
        both = rows(288 + 32 * q, 32)
        down_grad[2 * q] = both[:, :64]
        down_grad[2 * q + 1] = pltpu.roll(both, 64, 1)[:, :64]


def call(kernel, outs, arrays, scratch=(), far=0, name=None):
    arrays = [pltpu.with_memory_space_constraint(a, pltpu.HBM) for a in arrays[:far]] + arrays[far:]
    spaces = [pltpu.HBM] * far + [pltpu.VMEM] * (len(arrays) - far)
    return pl.pallas_call(
        kernel,
        out_shape=[jax.ShapeDtypeStruct(shape, dtype) for shape, dtype in outs],
        in_specs=[pl.BlockSpec(memory_space=space) for space in spaces],
        out_specs=[pl.BlockSpec(memory_space=pltpu.VMEM)] * len(outs),
        scratch_shapes=scratch,
        compiler_params=pltpu.CompilerParams(vmem_limit_bytes=40 * 2**20),
        name=name,
    )(*arrays)


def shards(features, active, coarse_grad, conv_weight, down_weight):
    fine = features[0]
    devices = lax.axis_size(BLOCKS)
    scale = (lax.axis_size("vol") * devices * fine.size // 32) ** -0.5
    full = WIDE + ROW
    to_next, to_prev, coarse, live, fine, conv, down = call(
        pack_kernel,
        [
            ((8, 2560), BF16), ((8, 2560), BF16), ((128, ROW), BF16), ((8, ROW), F32),
            (fine.shape, BF16), (conv_weight.shape, BF16), (down_weight.shape, BF16),
        ],
        [active, fine, coarse_grad[0], conv_weight, down_weight],
        [
            pltpu.SMEM(active.shape, jnp.int32),
            pltpu.VMEM(coarse_grad.shape[1:], BF16),
            pltpu.SemaphoreType.DMA((7,)),
        ],
        far=5, name="pack",
    )
    up = [(i, i + 1) for i in range(devices - 1)]
    from_prev = lax.ppermute(to_next, BLOCKS, up)
    from_next = lax.ppermute(to_prev, BLOCKS, [(j, i) for i, j in up])
    outer, inner, bands, spread, dpre, dy, state = call(
        inner_kernel,
        [
            ((8, 80, full), BF16), ((8, 64, full), BF16), ((9, WIDE, ROW), BF16), ((ROW, 4 * ROW), BF16),
            ((6, 64, ROW), BF16), ((8, 64, ROW), F32), ((4, 128, ROW), BF16),
        ],
        [live, fine, conv, down, coarse],
        [pltpu.VMEM((384, ROW), F32), pltpu.VMEM((128, 4 * ROW), F32)],
        name="inner",
    )
    grads, dpre = call(
        lambda *refs: main_kernel(scale, *refs),
        [((512, 128), F32), ((10, 64, ROW), BF16)],
        [inner, outer, from_prev, from_next, coarse, bands, spread, dpre, dy, state],
        [
            pltpu.VMEM((12, 80, full), BF16), pltpu.VMEM((12, 64, full), BF16), pltpu.VMEM((2, 32, ROW), BF16),
            pltpu.VMEM((2, 128, ROW), F32), pltpu.VMEM((4, 128, ROW), BF16),
        ],
        name="main",
    )
    count, far = lax.axis_size(NEAR), lax.axis_size("z")
    pieces = 512 // PIECE
    cut = grads.reshape(count, pieces // count, PIECE, 128) if count != pieces else grads.reshape(count, PIECE, 128)
    cut = lax.all_to_all(cut, NEAR, 0, 0)
    (result,) = call(
        back_kernel, [((8, 64 * ROW), BF16)], [live, conv, dpre, dy],
        [
            pltpu.VMEM((10, 80, WIDE), BF16), pltpu.VMEM((10, 64, WIDE), BF16), pltpu.VMEM((9, WIDE, ROW), BF16),
        ],
        name="back",
    )
    (mine,) = call(sum_kernel, [((far,) + cut.shape[1:], F32)], [cut], name="sum_near")
    mine = lax.all_to_all(mine, "z", 0, 0)
    (mine,) = call(sum_kernel, [(cut.shape, BF16)], [mine], name="sum_far")
    whole = lax.all_to_all(mine, NEAR, 0, 0).reshape(pieces, PIECE, 128)
    conv_grad, down_grad = call(
        finish_kernel, [((27, 32, 32), F32), ((8, 32, 64), F32)], [whole], name="finish"
    )
    return result[None], conv_grad, down_grad


def solution(mesh):
    fine = Mesh(mesh.devices.reshape(-1, 4, 2, mesh.shape["vol"]), BLOCKS + ("vol",))
    placed = (P("vol", BLOCKS, None), P("vol", BLOCKS), P("vol", BLOCKS, None), P(), P())
    return jax.shard_map(
        shards,
        mesh=fine,
        in_specs=placed,
        out_specs=(P("vol", BLOCKS, None), P(), P()),
        check_vma=False,
    )
```

```python
import functools
import math

import jax
import jax.numpy as jnp
from jax import lax
from jax.experimental import pallas as pl
from jax.experimental.pallas import tpu as pltpu
from jax.sharding import Mesh
from jax.sharding import PartitionSpec as P

BLOCKS = ("z", "x", "core")
NEAR = ("x", "core", "vol")
F32 = jnp.float32
BF16 = jnp.bfloat16

ROW = 256
WIDE = 384
GRADS = 384
SENT = BF16


def iota(shape, dim):
    return lax.broadcasted_iota(jnp.int32, shape, dim)


def live_rows(active_ref):
    slot = iota((8, ROW), 0)
    out = jnp.zeros((8, ROW), F32)
    for b in range(8):
        out = jnp.where(slot == b, active_ref[0, b].astype(F32), out)
    return out


def repeat_lanes(rows, lanes):
    return (iota((rows, lanes), 1) % rows == iota((rows, lanes), 0)).astype(BF16)


def widen(row, halves):
    slot, lane = iota((8, 128), 0), iota((8, 128), 1)
    first, second = row[:, :128], row[:, 128:]
    right = pltpu.roll(first, 7, 0)
    left = pltpu.roll(second, 1, 0)
    edge = jnp.where(
        (slot % 2 == 0) & (lane < 32), right, jnp.where((slot % 2 == 1) & (lane >= 96), left, 0.0)
    )
    parts = [first, second, edge]
    if halves:
        parts += [jnp.where(lane >= 96, edge, second), jnp.where(lane < 32, edge, first)]
    return jnp.concatenate(parts, axis=1)


def put_plane(outer, inner, z, rows, halves=True):
    full = [widen(row, halves) for row in rows]
    upper = (iota(full[0].shape, 0) // 2) % 2
    low = jnp.where(upper == 1, pltpu.roll(full[7], 2, 0), 0.0)
    high = jnp.where(upper == 0, pltpu.roll(full[0], 6, 0), 0.0)
    ring = [low] + full + [high]
    for k in range(5):
        outer[z, 16 * k : 16 * k + 16] = jnp.concatenate(ring[2 * k : 2 * k + 2], 0).astype(BF16)
    for k in range(4):
        inner[z, 16 * k : 16 * k + 16] = jnp.concatenate(full[2 * k : 2 * k + 2], 0).astype(BF16)


def window(outer, inner, first, count, oz, oy, lanes):
    source = inner if oy == 1 else outer
    start = 16 if oy == 2 else 0
    rows = source[first + oz : first + oz + count, start : start + 64, lanes]
    return rows.reshape(count * 64, rows.shape[-1])


def convolve(outer, inner, bands, first, count):
    left = [
        window(outer, inner, first, count, index // 3, index % 3, slice(0, WIDE)) for index in range(9)
    ]
    return jnp.dot(
        jnp.concatenate(left, 1), bands[...].reshape(9 * WIDE, ROW), preferred_element_type=F32
    )


def slopes(pre, dy, fine):
    sig = 0.5 * jnp.tanh(0.5 * pre) + 0.5
    silu = pre * sig
    return (dy * sig * (1.0 + (pre - silu))).astype(BF16), fine + silu


def put_state(state, z, rows):
    for qy in range(2):
        for half in range(2):
            pair = [rows[2 * half + k][8 * qy : 8 * qy + 8] for k in range(2)]
            start = 32 * (z // 2) + 16 * half
            state[2 * (z % 2) + qy, start : start + 16] = jnp.concatenate(pair, 0).astype(BF16)


def put_bands(bands, index, taps):
    spot = iota((32, ROW), 1) // 32
    for i in range(8):
        part = jnp.zeros((32, ROW), F32)
        for ox in range(3):
            part = jnp.where(spot == i + 1 - ox, taps[ox], part)
        bands[index, 32 * i : 32 * i + 32] = part.astype(BF16)
    bands[index, 256:288] = jnp.where(spot == 7, taps[2], 0.0).astype(BF16)
    bands[index, 288:352] = jnp.zeros((64, ROW), BF16)
    bands[index, 352:384] = jnp.where(spot == 0, taps[0], 0.0).astype(BF16)


def pack_kernel(
    active, features, coarse, conv, down, to_core, to_chip, coarse_rows, live_out, fine_out, conv_out, down_out,
    flags, flat, sems,
):
    ends = [slice(0, 4096), slice(12288, 16384), slice(4096, 12288)]
    copies = [
        pltpu.make_async_copy(active, flags, sems.at[0]),
        pltpu.make_async_copy(coarse, flat, sems.at[1]),
    ]
    copies += [
        pltpu.make_async_copy(features.at[:, lanes], fine_out.at[:, lanes], sems.at[2 + k])
        for k, lanes in enumerate(ends)
    ]
    copies += [
        pltpu.make_async_copy(conv, conv_out, sems.at[5]),
        pltpu.make_async_copy(down, down_out, sems.at[6]),
    ]
    for copy in copies:
        copy.start()
    copies[0].wait()
    live = live_rows(flags)
    live_out[...] = live
    slot = iota((8, ROW), 0)
    copies[1].wait()

    def coarse_row(zc, yc):
        parts = []
        for b in range(8):
            start = ((((b // 4) * 4 + zc) * 8 + ((b // 2) % 2) * 4 + yc) * 2 + b % 2) * ROW
            parts.append(flat[:, start : start + ROW].astype(F32))
        return jnp.concatenate(parts, 0) * live

    ends = {}
    for zc in range(4):
        for half in range(2):
            both = [coarse_row(zc, 2 * half + k) for k in range(2)]
            start = 32 * zc + 16 * half
            coarse_rows[start : start + 16] = jnp.concatenate(both, 0).astype(BF16)
            ends[zc, half] = both
    second = lax.axis_index("core") == 1

    def send(start, to_next, to_prev):
        to_core[:, start : start + ROW] = jnp.where(second, to_prev, to_next).astype(BF16)
        to_chip[:, start : start + ROW] = jnp.where(second, to_next, to_prev).astype(BF16)

    for half in range(2):
        last, first = ends[3, half], ends[0, half]
        send(
            2048 + half * ROW,
            jnp.where(slot < 4, pltpu.roll(last[0], 4, 0), last[1]),
            jnp.where(slot < 4, first[1], pltpu.roll(first[0], 4, 0)),
        )

    def fine(z, y):
        start = (z * 8 + y) * ROW
        return fine_out[:, start : start + ROW].astype(F32) * live

    copies[2].wait()
    copies[3].wait()
    for y in range(8):
        send(
            y * ROW,
            jnp.where(slot < 4, pltpu.roll(fine(6, y), 4, 0), fine(7, y)),
            jnp.where(slot < 4, fine(1, y), pltpu.roll(fine(0, y), 4, 0)),
        )
    for copy in copies[4:]:
        copy.wait()


def inner_kernel(
    live_in, features, conv, down, coarse, outer, inner, bands, spread, dpre, dy, state, pre, spread_out,
):
    live = live_in[...]
    tile = repeat_lanes(32, ROW)
    spot = iota((64, ROW), 1) // 32
    for q in range(4):
        turned = [
            lax.dot_general(down[2 * q + ox], tile, (((0,), (0,)), ((), ())), preferred_element_type=F32)
            for ox in range(2)
        ]
        for cx in range(4):
            part = jnp.where(spot == 2 * cx, turned[0], jnp.where(spot == 2 * cx + 1, turned[1], 0.0))
            spread[64 * cx : 64 * cx + 64, ROW * q : ROW * q + ROW] = part.astype(BF16)
    spread_out[...] = jnp.dot(coarse[...], spread[...], preferred_element_type=F32)
    taps = jnp.dot(conv[...].reshape(27 * 32, 32), tile, preferred_element_type=F32)
    for index in range(9):
        put_bands(bands, index, [taps[96 * index + 32 * ox : 96 * index + 32 * ox + 32] for ox in range(3)])
    for z in range(8):
        rows = []
        for y in range(8):
            start = (z * 8 + y) * ROW
            rows.append(features[:, start : start + ROW].astype(F32) * live)
        put_plane(outer, inner, z, rows)
    pre[...] = convolve(outer, inner, bands, 0, 6)
    for z in range(8):
        qz, rows = z % 2, []
        for pair in range(4):
            part = slice(16 * pair, 16 * pair + 16)
            base = 32 * (z // 2) + 8 * pair
            lanes = [slice(ROW * (2 * qz + qy), ROW * (2 * qz + qy) + ROW) for qy in range(2)]
            spread_rows = jnp.concatenate([spread_out[base : base + 8, lane] for lane in lanes], 0)
            dy[z, part] = spread_rows
            if 1 <= z <= 6:
                start = 64 * (z - 1) + 16 * pair
                fine = inner[z, part, :ROW].astype(F32)
                dpre[z - 1, part], y = slopes(pre[start : start + 16], spread_rows, fine)
                rows.append(y)
        if rows:
            put_state(state, z, rows)
    for z in (0, 7):
        put_state(state, z, [jnp.zeros((16, ROW), F32)] * 4)


def main_kernel(
    scale, inner_own, outer_own, from_core, from_chip, coarse, bands, spread, dpre_own, dy, state_own,
    grads, dpre, outer, inner, ends, pre, state,
):
    slot = iota((8, ROW), 0)
    outer[2:10] = outer_own[...]
    inner[2:10] = inner_own[...]
    dpre[2:8] = dpre_own[...]
    state[...] = state_own[...]

    second = lax.axis_index("core") == 1

    def received(start):
        core = from_core[:, start : start + ROW].astype(F32)
        chip = from_chip[:, start : start + ROW].astype(F32)
        return jnp.where(second, core, chip), jnp.where(second, chip, core)

    def own(z, y):
        return inner_own[z, 16 * (y // 2) : 16 * (y // 2) + 16, :ROW].astype(F32)[8 * (y % 2) : 8 * (y % 2) + 8]

    before, beyond, after, past = [], [], [], []
    for y in range(8):
        low, high = received(y * ROW)
        beyond.append(jnp.where(slot < 4, low, pltpu.roll(own(6, y), 4, 0)))
        before.append(pltpu.roll(jnp.where(slot >= 4, low, own(7, y)), 4, 0))
        after.append(jnp.where(slot >= 4, high, pltpu.roll(own(0, y), 4, 0)))
        past.append(pltpu.roll(jnp.where(slot < 4, high, own(1, y)), 4, 0))
    for z, rows in ((0, beyond), (1, before), (10, after), (11, past)):
        put_plane(outer, inner, z, rows)

    for k in range(2):
        low, high = received(2048 + k * ROW)
        last = coarse[96 + 16 * k : 112 + 16 * k].astype(F32)
        first = coarse[16 * k : 16 * k + 16].astype(F32)
        under = [
            jnp.where(slot < 4, low, pltpu.roll(last[:8], 4, 0)),
            pltpu.roll(jnp.where(slot >= 4, low, last[8:]), 4, 0),
        ]
        over = [
            jnp.where(slot >= 4, high, pltpu.roll(first[:8], 4, 0)),
            pltpu.roll(jnp.where(slot < 4, high, first[8:]), 4, 0),
        ]
        ends[0, 16 * k : 16 * k + 16] = jnp.concatenate(under, 0).astype(BF16)
        ends[1, 16 * k : 16 * k + 16] = jnp.concatenate(over, 0).astype(BF16)
    dy_end = [
        jnp.dot(ends[0], spread[:, 2 * ROW :], preferred_element_type=F32),
        jnp.dot(ends[1], spread[:, : 2 * ROW], preferred_element_type=F32),
    ]

    for side in range(2):
        pre[side] = convolve(outer, inner, bands, 8 * side, 2)
    for side in range(2):
        for k in range(2):
            step = 8 * side + k
            z = step - 1
            rows = []
            for pair in range(4):
                part = slice(16 * pair, 16 * pair + 16)
                if 0 <= z < 8:
                    back = dy[z, part]
                else:
                    back = jnp.concatenate(
                        [dy_end[side][8 * pair : 8 * pair + 8, ROW * qy : ROW * qy + ROW] for qy in range(2)], 0
                    )
                start = 64 * k + 16 * pair
                fine = inner[step + 1, part, :ROW].astype(F32)
                dpre[step, part], y = slopes(pre[side, start : start + 16], back, fine)
                rows.append(y)
            if 0 <= z < 8:
                put_state(state, z, rows)

    lane = iota((32, 128), 1)
    v0, v1, low1, high1 = slice(0, 128), slice(128, 256), slice(384, 512), slice(512, 640)
    turned = dpre[1:9].reshape(512, ROW).T
    turned = jnp.concatenate([turned[:128], turned[128:]], 1)
    blocks = []
    for oz in range(3):
        right = []
        for oy in range(3):
            halves = [
                jnp.concatenate([window(outer, inner, 1, 8, oz, oy, part) for part in parts], 1)
                for parts in ((v0, low1), (v1, high1))
            ]
            right.append(jnp.concatenate(halves, 0))
        products = jnp.dot(turned, jnp.concatenate(right, 1), preferred_element_type=F32)
        for oy in range(3):
            block = [products[32 * j : 32 * j + 32, ROW * oy : ROW * oy + ROW] for j in range(4)]
            t0 = jnp.where(lane >= 96, block[0][:, v1], block[0][:, v0])
            t3 = jnp.where(lane < 32, block[3][:, v1], block[3][:, v0])
            folded = (
                pltpu.roll(t0, 32, 1)
                + block[1][:, v0]
                + pltpu.roll(block[2][:, v0], 96, 1)
                + pltpu.roll(t3, 64, 1)
            )
            blocks.append(jnp.where(lane < 96, folded * scale, 0.0))
    for index in range(8):
        both = blocks[index]
        if index < 3:
            both = jnp.where(lane < 96, both, pltpu.roll(blocks[8], 96 - 32 * index, 1))
        grads[32 * index : 32 * index + 32] = both.astype(SENT)
    left = jnp.concatenate(
        [jnp.concatenate([state[q][:, v0], state[q][:, v1]], 0) for q in range(4)], 1
    )
    right = jnp.concatenate([coarse[:, v0], coarse[:, v1]], 0)
    products = lax.dot_general(left, right, (((0,), (0,)), ((), ())), preferred_element_type=F32)
    for q in range(4):
        block = [products[128 * q + 32 * x : 128 * q + 32 * x + 32] for x in range(4)]
        folded = jnp.where(lane < 64, block[0], block[3]) + pltpu.roll(
            jnp.where(lane < 64, block[1], block[2]), 64, 1
        )
        grads[256 + 32 * q : 288 + 32 * q] = (folded * scale).astype(SENT)


def back_kernel(live_in, conv, dpre, dy, result, outer, inner, bands):
    live = live_in[...]
    tile = repeat_lanes(32, ROW)
    for index in range(9):
        taps = [
            lax.dot_general(
                conv[26 - (3 * index + ox)], tile, (((0,), (0,)), ((), ())), preferred_element_type=F32
            )
            for ox in range(3)
        ]
        put_bands(bands, index, taps)
    for z in range(10):
        rows = []
        for pair in range(4):
            both = dpre[z, 16 * pair : 16 * pair + 16].astype(F32)
            rows += [both[:8], both[8:]]
        put_plane(outer, inner, z, rows, halves=False)
    total = convolve(outer, inner, bands, 0, 8)
    for z in range(8):
        for y in range(8):
            row = 64 * z + 8 * y
            value = dy[z, 8 * y : 8 * y + 8] + live * total[row : row + 8]
            result[:, row * 32 : row * 32 + ROW] = value.astype(BF16)


def sum_kernel(piece, parts, out):
    unit = math.lcm(piece, 16)
    total = parts[:unit].astype(F32)
    for start in range(unit, parts.shape[0], unit):
        total = total + parts[start : start + unit].astype(F32)
    pieces = [total[start : start + piece] for start in range(0, unit, piece)]
    total = sum(pieces[1:], pieces[0])
    whole = jnp.concatenate([total] * len(pieces), 0).astype(out.dtype)
    for start in range(0, out.shape[0], unit):
        out[start : start + unit] = whole


def finish_kernel(whole, conv_grad, down_grad):
    for index in range(8):
        turned = whole[32 * index : 32 * index + 32].astype(F32).T
        for ox in range(3):
            conv_grad[3 * index + ox] = turned[32 * ox : 32 * ox + 32]
        if index < 3:
            conv_grad[24 + index] = turned[96:]
    for q in range(4):
        both = whole[256 + 32 * q : 288 + 32 * q].astype(F32)
        down_grad[2 * q] = both[:, :64]
        down_grad[2 * q + 1] = pltpu.roll(both, 64, 1)[:, :64]


def exchange(rows, axes):
    cut = rows.reshape(lax.axis_size(axes), -1, 4, 128)
    return lax.all_to_all(cut, axes, 0, 0).reshape(rows.shape)


def call(kernel, outs, arrays, scratch=(), far=0, name=None):
    arrays = [pltpu.with_memory_space_constraint(a, pltpu.HBM) for a in arrays[:far]] + arrays[far:]
    spaces = [pltpu.HBM] * far + [pltpu.VMEM] * (len(arrays) - far)
    return pl.pallas_call(
        kernel,
        out_shape=[jax.ShapeDtypeStruct(shape, dtype) for shape, dtype in outs],
        in_specs=[pl.BlockSpec(memory_space=space) for space in spaces],
        out_specs=[pl.BlockSpec(memory_space=pltpu.VMEM)] * len(outs),
        scratch_shapes=scratch,
        compiler_params=pltpu.CompilerParams(vmem_limit_bytes=40 * 2**20),
        name=name,
    )(*arrays)


def shards(features, active, coarse_grad, conv_weight, down_weight):
    fine = features[0]
    devices = lax.axis_size(BLOCKS)
    scale = (lax.axis_size("vol") * devices * fine.size // 32) ** -0.5
    full = WIDE + ROW
    to_core, to_chip, coarse, live, fine, conv, down = call(
        pack_kernel,
        [
            ((8, 2560), BF16), ((8, 2560), BF16), ((128, ROW), BF16), ((8, ROW), F32),
            (fine.shape, BF16), (conv_weight.shape, BF16), (down_weight.shape, BF16),
        ],
        [active, fine, coarse_grad[0], conv_weight, down_weight],
        [
            pltpu.SMEM(active.shape, jnp.int32),
            pltpu.VMEM(coarse_grad.shape[1:], BF16),
            pltpu.SemaphoreType.DMA((7,)),
        ],
        far=5, name="pack",
    )
    pairs = [(i, i + 1) for i in range(1, devices - 1, 2)]
    from_chip = lax.ppermute(to_chip, BLOCKS, pairs + [(j, i) for i, j in pairs])
    from_core = lax.ppermute(to_core, "core", [(0, 1), (1, 0)])
    outer, inner, bands, spread, dpre, dy, state = call(
        inner_kernel,
        [
            ((8, 80, full), BF16), ((8, 64, full), BF16), ((9, WIDE, ROW), BF16), ((ROW, 4 * ROW), BF16),
            ((6, 64, ROW), BF16), ((8, 64, ROW), F32), ((4, 128, ROW), BF16),
        ],
        [live, fine, conv, down, coarse],
        [pltpu.VMEM((384, ROW), F32), pltpu.VMEM((128, 4 * ROW), F32)],
        name="inner",
    )
    grads, dpre = call(
        lambda *refs: main_kernel(scale, *refs),
        [((GRADS, 128), SENT), ((10, 64, ROW), BF16)],
        [inner, outer, from_core, from_chip, coarse, bands, spread, dpre, dy, state],
        [
            pltpu.VMEM((12, 80, full), BF16), pltpu.VMEM((12, 64, full), BF16), pltpu.VMEM((2, 32, ROW), BF16),
            pltpu.VMEM((2, 128, ROW), F32), pltpu.VMEM((4, 128, ROW), BF16),
        ],
        name="main",
    )
    near, far = lax.axis_size(NEAR), lax.axis_size("z")
    add = functools.partial(sum_kernel, GRADS // near)
    parts = exchange(grads, NEAR)
    (result,) = call(
        back_kernel, [((8, 64 * ROW), BF16)], [live, conv, dpre, dy],
        [
            pltpu.VMEM((10, 80, WIDE), BF16), pltpu.VMEM((10, 64, WIDE), BF16), pltpu.VMEM((9, WIDE, ROW), BF16),
        ],
        name="back",
    )
    (sums,) = call(add, [((far * GRADS // near, 128), SENT)], [parts], name="sum_near")
    (sums,) = call(add, [((GRADS, 128), SENT)], [exchange(sums, "z")], name="sum_far")
    conv_grad, down_grad = call(
        finish_kernel, [((27, 32, 32), F32), ((8, 32, 64), F32)], [exchange(sums, NEAR)], name="finish"
    )
    return result[None], conv_grad, down_grad


def solution(mesh):
    fine = Mesh(mesh.devices.reshape(-1, 4, 2, mesh.shape["vol"]), BLOCKS + ("vol",))
    placed = (P("vol", BLOCKS, None), P("vol", BLOCKS), P("vol", BLOCKS, None), P(), P())
    return jax.shard_map(
        shards,
        mesh=fine,
        in_specs=placed,
        out_specs=(P("vol", BLOCKS, None), P(), P()),
        check_vma=False,
    )
```

```python
import functools
import math

import jax
import jax.numpy as jnp
from jax import lax
from jax.experimental import pallas as pl
from jax.experimental.pallas import tpu as pltpu
from jax.sharding import Mesh
from jax.sharding import PartitionSpec as P

BLOCKS = ("z", "x", "core")
NEAR = ("x", "core", "vol")
F32 = jnp.float32
BF16 = jnp.bfloat16

ROW = 256
WIDE = 384
GRADS = 384
SENT = BF16


def iota(shape, dim):
    return lax.broadcasted_iota(jnp.int32, shape, dim)


def live_rows(active_ref):
    slot = iota((8, ROW), 0)
    out = jnp.zeros((8, ROW), F32)
    for b in range(8):
        out = jnp.where(slot == b, active_ref[0, b].astype(F32), out)
    return out


def repeat_lanes(rows, lanes):
    return (iota((rows, lanes), 1) % rows == iota((rows, lanes), 0)).astype(BF16)


def widen(row, halves):
    slot, lane = iota((8, 128), 0), iota((8, 128), 1)
    first, second = row[:, :128], row[:, 128:]
    right = pltpu.roll(first, 7, 0)
    left = pltpu.roll(second, 1, 0)
    edge = jnp.where(
        (slot % 2 == 0) & (lane < 32), right, jnp.where((slot % 2 == 1) & (lane >= 96), left, 0.0)
    )
    parts = [first, second, edge]
    if halves:
        parts += [jnp.where(lane >= 96, edge, second), jnp.where(lane < 32, edge, first)]
    return jnp.concatenate(parts, axis=1)


def put_plane(outer, inner, z, rows, halves=True):
    full = [widen(row, halves) for row in rows]
    upper = (iota(full[0].shape, 0) // 2) % 2
    low = jnp.where(upper == 1, pltpu.roll(full[7], 2, 0), 0.0)
    high = jnp.where(upper == 0, pltpu.roll(full[0], 6, 0), 0.0)
    ring = [low] + full + [high]
    for k in range(5):
        outer[z, 16 * k : 16 * k + 16] = jnp.concatenate(ring[2 * k : 2 * k + 2], 0).astype(BF16)
    for k in range(4):
        inner[z, 16 * k : 16 * k + 16] = jnp.concatenate(full[2 * k : 2 * k + 2], 0).astype(BF16)


def window(outer, inner, first, count, oz, oy, lanes):
    source = inner if oy == 1 else outer
    start = 16 if oy == 2 else 0
    rows = source[first + oz : first + oz + count, start : start + 64, lanes]
    return rows.reshape(count * 64, rows.shape[-1])


def convolve(outer, inner, bands, first, count):
    left = [
        window(outer, inner, first, count, index // 3, index % 3, slice(0, WIDE)) for index in range(9)
    ]
    return jnp.dot(
        jnp.concatenate(left, 1), bands[...].reshape(9 * WIDE, ROW), preferred_element_type=F32
    )


def slopes(pre, dy, fine):
    sig = 0.5 * jnp.tanh(0.5 * pre) + 0.5
    silu = pre * sig
    return (dy * sig * (1.0 + (pre - silu))).astype(BF16), fine + silu


def put_state(state, z, rows):
    for qy in range(2):
        for half in range(2):
            pair = [rows[2 * half + k][8 * qy : 8 * qy + 8] for k in range(2)]
            start = 32 * (z // 2) + 16 * half
            state[2 * (z % 2) + qy, start : start + 16] = jnp.concatenate(pair, 0).astype(BF16)


def put_bands(bands, index, taps):
    spot = iota((32, ROW), 1) // 32
    for i in range(8):
        part = jnp.zeros((32, ROW), F32)
        for ox in range(3):
            part = jnp.where(spot == i + 1 - ox, taps[ox], part)
        bands[index, 32 * i : 32 * i + 32] = part.astype(BF16)
    bands[index, 256:288] = jnp.where(spot == 7, taps[2], 0.0).astype(BF16)
    bands[index, 288:352] = jnp.zeros((64, ROW), BF16)
    bands[index, 352:384] = jnp.where(spot == 0, taps[0], 0.0).astype(BF16)


def pack_kernel(
    active, features, coarse, conv, down, to_core, to_chip, coarse_rows, live_out, fine_out, conv_out, down_out,
    flags, flat, sems,
):
    ends = [slice(0, 4096), slice(12288, 16384), slice(4096, 12288)]
    copies = [
        pltpu.make_async_copy(active, flags, sems.at[0]),
        pltpu.make_async_copy(coarse, flat, sems.at[1]),
    ]
    copies += [
        pltpu.make_async_copy(features.at[:, lanes], fine_out.at[:, lanes], sems.at[2 + k])
        for k, lanes in enumerate(ends)
    ]
    copies += [
        pltpu.make_async_copy(conv, conv_out, sems.at[5]),
        pltpu.make_async_copy(down, down_out, sems.at[6]),
    ]
    for copy in copies:
        copy.start()
    copies[0].wait()
    live = live_rows(flags)
    live_out[...] = live
    slot = iota((8, ROW), 0)
    copies[1].wait()

    def coarse_row(zc, yc):
        parts = []
        for b in range(8):
            start = ((((b // 4) * 4 + zc) * 8 + ((b // 2) % 2) * 4 + yc) * 2 + b % 2) * ROW
            parts.append(flat[:, start : start + ROW].astype(F32))
        return jnp.concatenate(parts, 0) * live

    ends = {}
    for zc in range(4):
        for half in range(2):
            both = [coarse_row(zc, 2 * half + k) for k in range(2)]
            start = 32 * zc + 16 * half
            coarse_rows[start : start + 16] = jnp.concatenate(both, 0).astype(BF16)
            ends[zc, half] = both
    second = lax.axis_index("core") == 1

    def send(start, to_next, to_prev):
        to_core[:, start : start + ROW] = jnp.where(second, to_prev, to_next).astype(BF16)
        to_chip[:, start : start + ROW] = jnp.where(second, to_next, to_prev).astype(BF16)

    for half in range(2):
        last, first = ends[3, half], ends[0, half]
        send(
            2048 + half * ROW,
            jnp.where(slot < 4, pltpu.roll(last[0], 4, 0), last[1]),
            jnp.where(slot < 4, first[1], pltpu.roll(first[0], 4, 0)),
        )

    def fine(z, y):
        start = (z * 8 + y) * ROW
        return fine_out[:, start : start + ROW].astype(F32) * live

    copies[2].wait()
    copies[3].wait()
    for y in range(8):
        send(
            y * ROW,
            jnp.where(slot < 4, pltpu.roll(fine(6, y), 4, 0), fine(7, y)),
            jnp.where(slot < 4, fine(1, y), pltpu.roll(fine(0, y), 4, 0)),
        )
    for copy in copies[4:]:
        copy.wait()


def inner_kernel(
    live_in, features, conv, down, coarse, outer, inner, bands, spread, dpre, dy, state, pre, spread_out,
):
    live = live_in[...]
    tile = repeat_lanes(32, ROW)
    spot = iota((64, ROW), 1) // 32
    for q in range(4):
        turned = [
            lax.dot_general(down[2 * q + ox], tile, (((0,), (0,)), ((), ())), preferred_element_type=F32)
            for ox in range(2)
        ]
        for cx in range(4):
            part = jnp.where(spot == 2 * cx, turned[0], jnp.where(spot == 2 * cx + 1, turned[1], 0.0))
            spread[64 * cx : 64 * cx + 64, ROW * q : ROW * q + ROW] = part.astype(BF16)
    spread_out[...] = jnp.dot(coarse[...], spread[...], preferred_element_type=F32)
    taps = jnp.dot(conv[...].reshape(27 * 32, 32), tile, preferred_element_type=F32)
    for index in range(9):
        put_bands(bands, index, [taps[96 * index + 32 * ox : 96 * index + 32 * ox + 32] for ox in range(3)])
    for z in range(8):
        rows = []
        for y in range(8):
            start = (z * 8 + y) * ROW
            rows.append(features[:, start : start + ROW].astype(F32) * live)
        put_plane(outer, inner, z, rows)
    pre[...] = convolve(outer, inner, bands, 0, 6)
    for z in range(8):
        qz, rows = z % 2, []
        for pair in range(4):
            part = slice(16 * pair, 16 * pair + 16)
            base = 32 * (z // 2) + 8 * pair
            lanes = [slice(ROW * (2 * qz + qy), ROW * (2 * qz + qy) + ROW) for qy in range(2)]
            spread_rows = jnp.concatenate([spread_out[base : base + 8, lane] for lane in lanes], 0)
            dy[z, part] = spread_rows
            if 1 <= z <= 6:
                start = 64 * (z - 1) + 16 * pair
                fine = inner[z, part, :ROW].astype(F32)
                dpre[z - 1, part], y = slopes(pre[start : start + 16], spread_rows, fine)
                rows.append(y)
        if rows:
            put_state(state, z, rows)
    for z in (0, 7):
        put_state(state, z, [jnp.zeros((16, ROW), F32)] * 4)


def main_kernel(
    scale, inner_own, outer_own, from_chip, from_core, coarse, bands, spread, dpre_own, dy, state_own,
    grads, dpre, outer, inner, ends, pre, state,
):
    slot = iota((8, ROW), 0)
    outer[2:10] = outer_own[...]
    inner[2:10] = inner_own[...]
    dpre[2:8] = dpre_own[...]
    state[...] = state_own[...]

    second = lax.axis_index("core") == 1

    def received(start):
        core = from_core[:, start : start + ROW].astype(F32)
        chip = from_chip[:, start : start + ROW].astype(F32)
        return jnp.where(second, core, chip), jnp.where(second, chip, core)

    def own(z, y):
        return inner_own[z, 16 * (y // 2) : 16 * (y // 2) + 16, :ROW].astype(F32)[8 * (y % 2) : 8 * (y % 2) + 8]

    before, beyond, after, past = [], [], [], []
    for y in range(8):
        low, high = received(y * ROW)
        beyond.append(jnp.where(slot < 4, low, pltpu.roll(own(6, y), 4, 0)))
        before.append(pltpu.roll(jnp.where(slot >= 4, low, own(7, y)), 4, 0))
        after.append(jnp.where(slot >= 4, high, pltpu.roll(own(0, y), 4, 0)))
        past.append(pltpu.roll(jnp.where(slot < 4, high, own(1, y)), 4, 0))
    for z, rows in ((0, beyond), (1, before), (10, after), (11, past)):
        put_plane(outer, inner, z, rows)

    for k in range(2):
        low, high = received(2048 + k * ROW)
        last = coarse[96 + 16 * k : 112 + 16 * k].astype(F32)
        first = coarse[16 * k : 16 * k + 16].astype(F32)
        under = [
            jnp.where(slot < 4, low, pltpu.roll(last[:8], 4, 0)),
            pltpu.roll(jnp.where(slot >= 4, low, last[8:]), 4, 0),
        ]
        over = [
            jnp.where(slot >= 4, high, pltpu.roll(first[:8], 4, 0)),
            pltpu.roll(jnp.where(slot < 4, high, first[8:]), 4, 0),
        ]
        ends[0, 16 * k : 16 * k + 16] = jnp.concatenate(under, 0).astype(BF16)
        ends[1, 16 * k : 16 * k + 16] = jnp.concatenate(over, 0).astype(BF16)
    dy_end = [
        jnp.dot(ends[0], spread[:, 2 * ROW :], preferred_element_type=F32),
        jnp.dot(ends[1], spread[:, : 2 * ROW], preferred_element_type=F32),
    ]

    for side in range(2):
        pre[side] = convolve(outer, inner, bands, 8 * side, 2)
    for side in range(2):
        for k in range(2):
            step = 8 * side + k
            z = step - 1
            rows = []
            for pair in range(4):
                part = slice(16 * pair, 16 * pair + 16)
                if 0 <= z < 8:
                    back = dy[z, part]
                else:
                    back = jnp.concatenate(
                        [dy_end[side][8 * pair : 8 * pair + 8, ROW * qy : ROW * qy + ROW] for qy in range(2)], 0
                    )
                start = 64 * k + 16 * pair
                fine = inner[step + 1, part, :ROW].astype(F32)
                dpre[step, part], y = slopes(pre[side, start : start + 16], back, fine)
                rows.append(y)
            if 0 <= z < 8:
                put_state(state, z, rows)

    lane = iota((32, 128), 1)
    v0, v1, low1, high1 = slice(0, 128), slice(128, 256), slice(384, 512), slice(512, 640)
    turned = dpre[1:9].reshape(512, ROW).T
    turned = jnp.concatenate([turned[:128], turned[128:]], 1)
    blocks = []
    for oz in range(3):
        right = []
        for oy in range(3):
            halves = [
                jnp.concatenate([window(outer, inner, 1, 8, oz, oy, part) for part in parts], 1)
                for parts in ((v0, low1), (v1, high1))
            ]
            right.append(jnp.concatenate(halves, 0))
        products = jnp.dot(turned, jnp.concatenate(right, 1), preferred_element_type=F32)
        for oy in range(3):
            block = [products[32 * j : 32 * j + 32, ROW * oy : ROW * oy + ROW] for j in range(4)]
            t0 = jnp.where(lane >= 96, block[0][:, v1], block[0][:, v0])
            t3 = jnp.where(lane < 32, block[3][:, v1], block[3][:, v0])
            folded = (
                pltpu.roll(t0, 32, 1)
                + block[1][:, v0]
                + pltpu.roll(block[2][:, v0], 96, 1)
                + pltpu.roll(t3, 64, 1)
            )
            blocks.append(jnp.where(lane < 96, folded * scale, 0.0))
    for index in range(8):
        both = blocks[index]
        if index < 3:
            both = jnp.where(lane < 96, both, pltpu.roll(blocks[8], 96 - 32 * index, 1))
        grads[32 * index : 32 * index + 32] = both.astype(SENT)
    left = jnp.concatenate(
        [jnp.concatenate([state[q][:, v0], state[q][:, v1]], 0) for q in range(4)], 1
    )
    right = jnp.concatenate([coarse[:, v0], coarse[:, v1]], 0)
    products = lax.dot_general(left, right, (((0,), (0,)), ((), ())), preferred_element_type=F32)
    for q in range(4):
        block = [products[128 * q + 32 * x : 128 * q + 32 * x + 32] for x in range(4)]
        folded = jnp.where(lane < 64, block[0], block[3]) + pltpu.roll(
            jnp.where(lane < 64, block[1], block[2]), 64, 1
        )
        grads[256 + 32 * q : 288 + 32 * q] = (folded * scale).astype(SENT)


def back_kernel(live_in, conv, dpre, dy, result, outer, inner, bands):
    live = live_in[...]
    tile = repeat_lanes(32, ROW)
    for index in range(9):
        taps = [
            lax.dot_general(
                conv[26 - (3 * index + ox)], tile, (((0,), (0,)), ((), ())), preferred_element_type=F32
            )
            for ox in range(3)
        ]
        put_bands(bands, index, taps)
    for z in range(10):
        rows = []
        for pair in range(4):
            both = dpre[z, 16 * pair : 16 * pair + 16].astype(F32)
            rows += [both[:8], both[8:]]
        put_plane(outer, inner, z, rows, halves=False)
    total = convolve(outer, inner, bands, 0, 8)
    for z in range(8):
        for y in range(8):
            row = 64 * z + 8 * y
            value = dy[z, 8 * y : 8 * y + 8] + live * total[row : row + 8]
            result[:, row * 32 : row * 32 + ROW] = value.astype(BF16)


def sum_kernel(piece, parts, out):
    unit = math.lcm(piece, 16)
    total = parts[:unit].astype(F32)
    for start in range(unit, parts.shape[0], unit):
        total = total + parts[start : start + unit].astype(F32)
    pieces = [total[start : start + piece] for start in range(0, unit, piece)]
    total = sum(pieces[1:], pieces[0])
    whole = jnp.concatenate([total] * len(pieces), 0).astype(out.dtype)
    for start in range(0, out.shape[0], unit):
        out[start : start + unit] = whole


def finish_kernel(whole, conv_grad, down_grad):
    for index in range(8):
        turned = whole[32 * index : 32 * index + 32].astype(F32).T
        for ox in range(3):
            conv_grad[3 * index + ox] = turned[32 * ox : 32 * ox + 32]
        if index < 3:
            conv_grad[24 + index] = turned[96:]
    for q in range(4):
        both = whole[256 + 32 * q : 288 + 32 * q].astype(F32)
        down_grad[2 * q] = both[:, :64]
        down_grad[2 * q + 1] = pltpu.roll(both, 64, 1)[:, :64]


def exchange(rows, axes):
    cut = rows.reshape(lax.axis_size(axes), -1, 4, 128)
    return lax.all_to_all(cut, axes, 0, 0).reshape(rows.shape)


def call(kernel, outs, arrays, scratch=(), far=0, name=None):
    arrays = [pltpu.with_memory_space_constraint(a, pltpu.HBM) for a in arrays[:far]] + arrays[far:]
    spaces = [pltpu.HBM] * far + [pltpu.VMEM] * (len(arrays) - far)
    return pl.pallas_call(
        kernel,
        out_shape=[jax.ShapeDtypeStruct(shape, dtype) for shape, dtype in outs],
        in_specs=[pl.BlockSpec(memory_space=space) for space in spaces],
        out_specs=[pl.BlockSpec(memory_space=pltpu.VMEM)] * len(outs),
        scratch_shapes=scratch,
        compiler_params=pltpu.CompilerParams(vmem_limit_bytes=40 * 2**20),
        name=name,
    )(*arrays)


def shards(features, active, coarse_grad, conv_weight, down_weight):
    fine = features[0]
    devices = lax.axis_size(BLOCKS)
    scale = (lax.axis_size("vol") * devices * fine.size // 32) ** -0.5
    full = WIDE + ROW
    to_core, to_chip, coarse, live, fine, conv, down = call(
        pack_kernel,
        [
            ((8, 2560), BF16), ((8, 2560), BF16), ((128, ROW), BF16), ((8, ROW), F32),
            (fine.shape, BF16), (conv_weight.shape, BF16), (down_weight.shape, BF16),
        ],
        [active, fine, coarse_grad[0], conv_weight, down_weight],
        [
            pltpu.SMEM(active.shape, jnp.int32),
            pltpu.VMEM(coarse_grad.shape[1:], BF16),
            pltpu.SemaphoreType.DMA((7,)),
        ],
        far=5, name="pack",
    )
    pairs = [(i, i + 1) for i in range(1, devices - 1, 2)]
    from_chip = lax.ppermute(to_chip, BLOCKS, pairs + [(j, i) for i, j in pairs])
    from_core = lax.ppermute(to_core, "core", [(0, 1), (1, 0)])
    outer, inner, bands, spread, dpre, dy, state = call(
        inner_kernel,
        [
            ((8, 80, full), BF16), ((8, 64, full), BF16), ((9, WIDE, ROW), BF16), ((ROW, 4 * ROW), BF16),
            ((6, 64, ROW), BF16), ((8, 64, ROW), F32), ((4, 128, ROW), BF16),
        ],
        [live, fine, conv, down, coarse],
        [pltpu.VMEM((384, ROW), F32), pltpu.VMEM((128, 4 * ROW), F32)],
        name="inner",
    )
    grads, dpre = call(
        lambda *refs: main_kernel(scale, *refs),
        [((GRADS, 128), SENT), ((10, 64, ROW), BF16)],
        [inner, outer, from_chip, from_core, coarse, bands, spread, dpre, dy, state],
        [
            pltpu.VMEM((12, 80, full), BF16), pltpu.VMEM((12, 64, full), BF16), pltpu.VMEM((2, 32, ROW), BF16),
            pltpu.VMEM((2, 128, ROW), F32), pltpu.VMEM((4, 128, ROW), BF16),
        ],
        name="main",
    )
    near, far = lax.axis_size(NEAR), lax.axis_size("z")
    add = functools.partial(sum_kernel, GRADS // near)
    parts = exchange(grads, NEAR)
    (result,) = call(
        back_kernel, [((8, 64 * ROW), BF16)], [live, conv, dpre, dy],
        [
            pltpu.VMEM((10, 80, WIDE), BF16), pltpu.VMEM((10, 64, WIDE), BF16), pltpu.VMEM((9, WIDE, ROW), BF16),
        ],
        name="back",
    )
    (sums,) = call(add, [((far * GRADS // near, 128), SENT)], [parts], name="sum_near")
    (sums,) = call(add, [((GRADS, 128), SENT)], [exchange(sums, "z")], name="sum_far")
    conv_grad, down_grad = call(
        finish_kernel, [((27, 32, 32), F32), ((8, 32, 64), F32)], [exchange(sums, NEAR)], name="finish"
    )
    return result[None], conv_grad, down_grad


def solution(mesh):
    fine = Mesh(mesh.devices.reshape(-1, 4, 2, mesh.shape["vol"]), BLOCKS + ("vol",))
    placed = (P("vol", BLOCKS, None), P("vol", BLOCKS), P("vol", BLOCKS, None), P(), P())
    return jax.shard_map(
        shards,
        mesh=fine,
        in_specs=placed,
        out_specs=(P("vol", BLOCKS, None), P(), P()),
        check_vma=False,
    )
```

```python
import functools
import math

import jax
import jax.numpy as jnp
from jax import lax
from jax.experimental import pallas as pl
from jax.experimental.pallas import tpu as pltpu
from jax.sharding import Mesh
from jax.sharding import PartitionSpec as P

BLOCKS = ("z", "x", "core")
NEAR = ("x", "core", "vol")
F32 = jnp.float32
BF16 = jnp.bfloat16

ROW = 256
WIDE = 384
GRADS = 384
SENT = BF16


def iota(shape, dim):
    return lax.broadcasted_iota(jnp.int32, shape, dim)


def live_rows(active_ref):
    slot = iota((8, ROW), 0)
    out = jnp.zeros((8, ROW), F32)
    for b in range(8):
        out = jnp.where(slot == b, active_ref[0, b].astype(F32), out)
    return out


def repeat_lanes(rows, lanes):
    return (iota((rows, lanes), 1) % rows == iota((rows, lanes), 0)).astype(BF16)


def widen(row, halves):
    slot, lane = iota((8, 128), 0), iota((8, 128), 1)
    first, second = row[:, :128], row[:, 128:]
    right = pltpu.roll(first, 7, 0)
    left = pltpu.roll(second, 1, 0)
    edge = jnp.where(
        (slot % 2 == 0) & (lane < 32), right, jnp.where((slot % 2 == 1) & (lane >= 96), left, 0.0)
    )
    parts = [first, second, edge]
    if halves:
        parts += [jnp.where(lane >= 96, edge, second), jnp.where(lane < 32, edge, first)]
    return jnp.concatenate(parts, axis=1)


def put_plane(outer, inner, z, rows, halves=True):
    full = [widen(row, halves) for row in rows]
    upper = (iota(full[0].shape, 0) // 2) % 2
    low = jnp.where(upper == 1, pltpu.roll(full[7], 2, 0), 0.0)
    high = jnp.where(upper == 0, pltpu.roll(full[0], 6, 0), 0.0)
    ring = [low] + full + [high]
    for k in range(5):
        outer[z, 16 * k : 16 * k + 16] = jnp.concatenate(ring[2 * k : 2 * k + 2], 0).astype(BF16)
    for k in range(4):
        inner[z, 16 * k : 16 * k + 16] = jnp.concatenate(full[2 * k : 2 * k + 2], 0).astype(BF16)


def window(outer, inner, first, count, oz, oy, lanes):
    source = inner if oy == 1 else outer
    start = 16 if oy == 2 else 0
    rows = source[first + oz : first + oz + count, start : start + 64, lanes]
    return rows.reshape(count * 64, rows.shape[-1])


def convolve(outer, inner, bands, first, count):
    left = [
        window(outer, inner, first, count, index // 3, index % 3, slice(0, WIDE)) for index in range(9)
    ]
    return jnp.dot(
        jnp.concatenate(left, 1), bands[...].reshape(9 * WIDE, ROW), preferred_element_type=F32
    )


def slopes(pre, dy, fine):
    sig = 0.5 * jnp.tanh(0.5 * pre) + 0.5
    silu = pre * sig
    return (dy * sig * (1.0 + (pre - silu))).astype(BF16), fine + silu


def put_state(state, z, rows):
    for qy in range(2):
        for half in range(2):
            pair = [rows[2 * half + k][8 * qy : 8 * qy + 8] for k in range(2)]
            start = 32 * (z // 2) + 16 * half
            state[2 * (z % 2) + qy, start : start + 16] = jnp.concatenate(pair, 0).astype(BF16)


def put_bands(bands, index, taps):
    spot = iota((32, ROW), 1) // 32
    for i in range(8):
        part = jnp.zeros((32, ROW), F32)
        for ox in range(3):
            part = jnp.where(spot == i + 1 - ox, taps[ox], part)
        bands[index, 32 * i : 32 * i + 32] = part.astype(BF16)
    bands[index, 256:288] = jnp.where(spot == 7, taps[2], 0.0).astype(BF16)
    bands[index, 288:352] = jnp.zeros((64, ROW), BF16)
    bands[index, 352:384] = jnp.where(spot == 0, taps[0], 0.0).astype(BF16)


def pack_kernel(
    active, features, coarse, conv, down, to_core, to_chip, coarse_rows, live_out, fine_out, conv_out, down_out,
    flags, flat, sems,
):
    ends = [slice(0, 4096), slice(12288, 16384), slice(4096, 12288)]
    copies = [
        pltpu.make_async_copy(active, flags, sems.at[0]),
        pltpu.make_async_copy(coarse, flat, sems.at[1]),
    ]
    copies += [
        pltpu.make_async_copy(features.at[:, lanes], fine_out.at[:, lanes], sems.at[2 + k])
        for k, lanes in enumerate(ends)
    ]
    copies += [
        pltpu.make_async_copy(conv, conv_out, sems.at[5]),
        pltpu.make_async_copy(down, down_out, sems.at[6]),
    ]
    for copy in copies:
        copy.start()
    copies[0].wait()
    live = live_rows(flags)
    live_out[...] = live
    slot = iota((8, ROW), 0)
    copies[1].wait()

    def coarse_row(zc, yc):
        parts = []
        for b in range(8):
            start = ((((b // 4) * 4 + zc) * 8 + ((b // 2) % 2) * 4 + yc) * 2 + b % 2) * ROW
            parts.append(flat[:, start : start + ROW].astype(F32))
        return jnp.concatenate(parts, 0) * live

    ends = {}
    for zc in range(4):
        for half in range(2):
            both = [coarse_row(zc, 2 * half + k) for k in range(2)]
            start = 32 * zc + 16 * half
            coarse_rows[start : start + 16] = jnp.concatenate(both, 0).astype(BF16)
            ends[zc, half] = both
    second = lax.axis_index("core") == 1

    def send(start, to_next, to_prev):
        to_core[:, start : start + ROW] = jnp.where(second, to_prev, to_next).astype(BF16)
        to_chip[:, start : start + ROW] = jnp.where(second, to_next, to_prev).astype(BF16)

    for half in range(2):
        last, first = ends[3, half], ends[0, half]
        send(
            2048 + half * ROW,
            jnp.where(slot < 4, pltpu.roll(last[0], 4, 0), last[1]),
            jnp.where(slot < 4, first[1], pltpu.roll(first[0], 4, 0)),
        )

    def fine(z, y):
        start = (z * 8 + y) * ROW
        return fine_out[:, start : start + ROW].astype(F32) * live

    copies[2].wait()
    copies[3].wait()
    for y in range(8):
        send(
            y * ROW,
            jnp.where(slot < 4, pltpu.roll(fine(6, y), 4, 0), fine(7, y)),
            jnp.where(slot < 4, fine(1, y), pltpu.roll(fine(0, y), 4, 0)),
        )
    for copy in copies[4:]:
        copy.wait()


def inner_kernel(
    live_in, features, conv, down, coarse, outer, inner, bands, spread, dpre, dy, state, pre, spread_out,
):
    live = live_in[...]
    tile = repeat_lanes(32, ROW)
    spot = iota((64, ROW), 1) // 32
    for q in range(4):
        turned = [
            lax.dot_general(down[2 * q + ox], tile, (((0,), (0,)), ((), ())), preferred_element_type=F32)
            for ox in range(2)
        ]
        for cx in range(4):
            part = jnp.where(spot == 2 * cx, turned[0], jnp.where(spot == 2 * cx + 1, turned[1], 0.0))
            spread[64 * cx : 64 * cx + 64, ROW * q : ROW * q + ROW] = part.astype(BF16)
    spread_out[...] = jnp.dot(coarse[...], spread[...], preferred_element_type=F32)
    taps = jnp.dot(conv[...].reshape(27 * 32, 32), tile, preferred_element_type=F32)
    for index in range(9):
        put_bands(bands, index, [taps[96 * index + 32 * ox : 96 * index + 32 * ox + 32] for ox in range(3)])
    for z in range(8):
        rows = []
        for y in range(8):
            start = (z * 8 + y) * ROW
            rows.append(features[:, start : start + ROW].astype(F32) * live)
        put_plane(outer, inner, z, rows)
    pre[...] = convolve(outer, inner, bands, 0, 6)
    for z in range(8):
        qz, rows = z % 2, []
        for pair in range(4):
            part = slice(16 * pair, 16 * pair + 16)
            base = 32 * (z // 2) + 8 * pair
            lanes = [slice(ROW * (2 * qz + qy), ROW * (2 * qz + qy) + ROW) for qy in range(2)]
            spread_rows = jnp.concatenate([spread_out[base : base + 8, lane] for lane in lanes], 0)
            dy[z, part] = spread_rows
            if 1 <= z <= 6:
                start = 64 * (z - 1) + 16 * pair
                fine = inner[z, part, :ROW].astype(F32)
                dpre[z - 1, part], y = slopes(pre[start : start + 16], spread_rows, fine)
                rows.append(y)
        if rows:
            put_state(state, z, rows)
    for z in (0, 7):
        put_state(state, z, [jnp.zeros((16, ROW), F32)] * 4)


def main_kernel(
    scale, inner_own, outer_own, from_chip, from_core, coarse, bands, spread, dpre_own, dy, state_own,
    grads, dpre, outer, inner, ends, pre, state,
):
    slot = iota((8, ROW), 0)
    outer[2:10] = outer_own[...]
    inner[2:10] = inner_own[...]
    dpre[2:8] = dpre_own[...]
    state[...] = state_own[...]

    second = lax.axis_index("core") == 1

    def received(start):
        core = from_core[:, start : start + ROW].astype(F32)
        chip = from_chip[:, start : start + ROW].astype(F32)
        return jnp.where(second, core, chip), jnp.where(second, chip, core)

    def own(z, y):
        return inner_own[z, 16 * (y // 2) : 16 * (y // 2) + 16, :ROW].astype(F32)[8 * (y % 2) : 8 * (y % 2) + 8]

    before, beyond, after, past = [], [], [], []
    for y in range(8):
        low, high = received(y * ROW)
        beyond.append(jnp.where(slot < 4, low, pltpu.roll(own(6, y), 4, 0)))
        before.append(pltpu.roll(jnp.where(slot >= 4, low, own(7, y)), 4, 0))
        after.append(jnp.where(slot >= 4, high, pltpu.roll(own(0, y), 4, 0)))
        past.append(pltpu.roll(jnp.where(slot < 4, high, own(1, y)), 4, 0))
    for z, rows in ((0, beyond), (1, before), (10, after), (11, past)):
        put_plane(outer, inner, z, rows)

    for k in range(2):
        low, high = received(2048 + k * ROW)
        last = coarse[96 + 16 * k : 112 + 16 * k].astype(F32)
        first = coarse[16 * k : 16 * k + 16].astype(F32)
        under = [
            jnp.where(slot < 4, low, pltpu.roll(last[:8], 4, 0)),
            pltpu.roll(jnp.where(slot >= 4, low, last[8:]), 4, 0),
        ]
        over = [
            jnp.where(slot >= 4, high, pltpu.roll(first[:8], 4, 0)),
            pltpu.roll(jnp.where(slot < 4, high, first[8:]), 4, 0),
        ]
        ends[0, 16 * k : 16 * k + 16] = jnp.concatenate(under, 0).astype(BF16)
        ends[1, 16 * k : 16 * k + 16] = jnp.concatenate(over, 0).astype(BF16)
    dy_end = [
        jnp.dot(ends[0], spread[:, 2 * ROW :], preferred_element_type=F32),
        jnp.dot(ends[1], spread[:, : 2 * ROW], preferred_element_type=F32),
    ]

    for side in range(2):
        pre[side] = convolve(outer, inner, bands, 8 * side, 2)
    for side in range(2):
        for k in range(2):
            step = 8 * side + k
            z = step - 1
            rows = []
            for pair in range(4):
                part = slice(16 * pair, 16 * pair + 16)
                if 0 <= z < 8:
                    back = dy[z, part]
                else:
                    back = jnp.concatenate(
                        [dy_end[side][8 * pair : 8 * pair + 8, ROW * qy : ROW * qy + ROW] for qy in range(2)], 0
                    )
                start = 64 * k + 16 * pair
                fine = inner[step + 1, part, :ROW].astype(F32)
                dpre[step, part], y = slopes(pre[side, start : start + 16], back, fine)
                rows.append(y)
            if 0 <= z < 8:
                put_state(state, z, rows)

    lane = iota((32, 128), 1)
    v0, v1, low1, high1 = slice(0, 128), slice(128, 256), slice(384, 512), slice(512, 640)
    turned = dpre[1:9].reshape(512, ROW).T
    turned = jnp.concatenate([turned[:128], turned[128:]], 1)
    blocks = []
    for oz in range(3):
        right = []
        for oy in range(3):
            halves = [
                jnp.concatenate([window(outer, inner, 1, 8, oz, oy, part) for part in parts], 1)
                for parts in ((v0, low1), (v1, high1))
            ]
            right.append(jnp.concatenate(halves, 0))
        products = jnp.dot(turned, jnp.concatenate(right, 1), preferred_element_type=F32)
        for oy in range(3):
            block = [products[32 * j : 32 * j + 32, ROW * oy : ROW * oy + ROW] for j in range(4)]
            t0 = jnp.where(lane >= 96, block[0][:, v1], block[0][:, v0])
            t3 = jnp.where(lane < 32, block[3][:, v1], block[3][:, v0])
            folded = (
                pltpu.roll(t0, 32, 1)
                + block[1][:, v0]
                + pltpu.roll(block[2][:, v0], 96, 1)
                + pltpu.roll(t3, 64, 1)
            )
            blocks.append(jnp.where(lane < 96, folded * scale, 0.0))
    for index in range(8):
        both = blocks[index]
        if index < 3:
            both = jnp.where(lane < 96, both, pltpu.roll(blocks[8], 96 - 32 * index, 1))
        grads[32 * index : 32 * index + 32] = both.astype(SENT)
    left = jnp.concatenate(
        [jnp.concatenate([state[q][:, v0], state[q][:, v1]], 0) for q in range(4)], 1
    )
    right = jnp.concatenate([coarse[:, v0], coarse[:, v1]], 0)
    products = lax.dot_general(left, right, (((0,), (0,)), ((), ())), preferred_element_type=F32)
    for q in range(4):
        block = [products[128 * q + 32 * x : 128 * q + 32 * x + 32] for x in range(4)]
        folded = jnp.where(lane < 64, block[0], block[3]) + pltpu.roll(
            jnp.where(lane < 64, block[1], block[2]), 64, 1
        )
        grads[256 + 32 * q : 288 + 32 * q] = (folded * scale).astype(SENT)


def back_kernel(live_in, conv, dpre, dy, result, outer, inner, bands):
    live = live_in[...]
    tile = repeat_lanes(32, ROW)
    for index in range(9):
        taps = [
            lax.dot_general(
                conv[26 - (3 * index + ox)], tile, (((0,), (0,)), ((), ())), preferred_element_type=F32
            )
            for ox in range(3)
        ]
        put_bands(bands, index, taps)
    for z in range(10):
        rows = []
        for pair in range(4):
            both = dpre[z, 16 * pair : 16 * pair + 16].astype(F32)
            rows += [both[:8], both[8:]]
        put_plane(outer, inner, z, rows, halves=False)
    total = convolve(outer, inner, bands, 0, 8)
    for z in range(8):
        for y in range(8):
            row = 64 * z + 8 * y
            value = dy[z, 8 * y : 8 * y + 8] + live * total[row : row + 8]
            result[:, row * 32 : row * 32 + ROW] = value.astype(BF16)


def sum_kernel(piece, parts, out):
    unit = math.lcm(piece, 16)
    total = parts[:unit].astype(F32)
    for start in range(unit, parts.shape[0], unit):
        total = total + parts[start : start + unit].astype(F32)
    pieces = [total[start : start + piece] for start in range(0, unit, piece)]
    total = sum(pieces[1:], pieces[0])
    whole = jnp.concatenate([total] * len(pieces), 0).astype(out.dtype)
    for start in range(0, out.shape[0], unit):
        out[start : start + unit] = whole


def finish_kernel(whole, conv_grad, down_grad):
    for index in range(8):
        turned = whole[32 * index : 32 * index + 32].astype(F32).T
        for ox in range(3):
            conv_grad[3 * index + ox] = turned[32 * ox : 32 * ox + 32]
        if index < 3:
            conv_grad[24 + index] = turned[96:]
    for q in range(4):
        both = whole[256 + 32 * q : 288 + 32 * q].astype(F32)
        down_grad[2 * q] = both[:, :64]
        down_grad[2 * q + 1] = pltpu.roll(both, 64, 1)[:, :64]


def exchange(rows, axes, groups=None):
    cut = rows.reshape(lax.axis_size(axes), -1, 4, 128)
    return lax.all_to_all(cut, axes, 0, 0, axis_index_groups=groups).reshape(rows.shape)


def call(kernel, outs, arrays, scratch=(), far=0, name=None):
    arrays = [pltpu.with_memory_space_constraint(a, pltpu.HBM) for a in arrays[:far]] + arrays[far:]
    spaces = [pltpu.HBM] * far + [pltpu.VMEM] * (len(arrays) - far)
    return pl.pallas_call(
        kernel,
        out_shape=[jax.ShapeDtypeStruct(shape, dtype) for shape, dtype in outs],
        in_specs=[pl.BlockSpec(memory_space=space) for space in spaces],
        out_specs=[pl.BlockSpec(memory_space=pltpu.VMEM)] * len(outs),
        scratch_shapes=scratch,
        compiler_params=pltpu.CompilerParams(vmem_limit_bytes=40 * 2**20),
        name=name,
    )(*arrays)


def opposite():
    sizes = [lax.axis_size(axis) for axis in NEAR]
    order = []
    for x in range(sizes[0]):
        for core in range(sizes[1]):
            for vol in range(sizes[2]):
                spot = (x + sizes[0] // 2) % sizes[0] * sizes[1] + (core + 1) % sizes[1]
                order.append(spot * sizes[2] + (vol + sizes[2] // 2) % sizes[2])
    return [order]


def shards(features, active, coarse_grad, conv_weight, down_weight):
    fine = features[0]
    devices = lax.axis_size(BLOCKS)
    scale = (lax.axis_size("vol") * devices * fine.size // 32) ** -0.5
    full = WIDE + ROW
    to_core, to_chip, coarse, live, fine, conv, down = call(
        pack_kernel,
        [
            ((8, 2560), BF16), ((8, 2560), BF16), ((128, ROW), BF16), ((8, ROW), F32),
            (fine.shape, BF16), (conv_weight.shape, BF16), (down_weight.shape, BF16),
        ],
        [active, fine, coarse_grad[0], conv_weight, down_weight],
        [
            pltpu.SMEM(active.shape, jnp.int32),
            pltpu.VMEM(coarse_grad.shape[1:], BF16),
            pltpu.SemaphoreType.DMA((7,)),
        ],
        far=5, name="pack",
    )
    pairs = [(i, i + 1) for i in range(1, devices - 1, 2)]
    from_chip = lax.ppermute(to_chip, BLOCKS, pairs + [(j, i) for i, j in pairs])
    from_core = lax.ppermute(to_core, "core", [(0, 1), (1, 0)])
    outer, inner, bands, spread, dpre, dy, state = call(
        inner_kernel,
        [
            ((8, 80, full), BF16), ((8, 64, full), BF16), ((9, WIDE, ROW), BF16), ((ROW, 4 * ROW), BF16),
            ((6, 64, ROW), BF16), ((8, 64, ROW), F32), ((4, 128, ROW), BF16),
        ],
        [live, fine, conv, down, coarse],
        [pltpu.VMEM((384, ROW), F32), pltpu.VMEM((128, 4 * ROW), F32)],
        name="inner",
    )
    grads, dpre = call(
        lambda *refs: main_kernel(scale, *refs),
        [((GRADS, 128), SENT), ((10, 64, ROW), BF16)],
        [inner, outer, from_chip, from_core, coarse, bands, spread, dpre, dy, state],
        [
            pltpu.VMEM((12, 80, full), BF16), pltpu.VMEM((12, 64, full), BF16), pltpu.VMEM((2, 32, ROW), BF16),
            pltpu.VMEM((2, 128, ROW), F32), pltpu.VMEM((4, 128, ROW), BF16),
        ],
        name="main",
    )
    near, far = lax.axis_size(NEAR), lax.axis_size("z")
    plane = opposite()
    add = functools.partial(sum_kernel, GRADS // near)
    parts = exchange(grads, NEAR, plane)
    (result,) = call(
        back_kernel, [((8, 64 * ROW), BF16)], [live, conv, dpre, dy],
        [
            pltpu.VMEM((10, 80, WIDE), BF16), pltpu.VMEM((10, 64, WIDE), BF16), pltpu.VMEM((9, WIDE, ROW), BF16),
        ],
        name="back",
    )
    (sums,) = call(add, [((far * GRADS // near, 128), SENT)], [parts], name="sum_near")
    (sums,) = call(add, [((GRADS, 128), SENT)], [exchange(sums, "z", [[(k + far // 2) % far for k in range(far)]])], name="sum_far")
    conv_grad, down_grad = call(
        finish_kernel, [((27, 32, 32), F32), ((8, 32, 64), F32)], [exchange(sums, NEAR, plane)], name="finish"
    )
    return result[None], conv_grad, down_grad


def solution(mesh):
    fine = Mesh(mesh.devices.reshape(-1, 4, 2, mesh.shape["vol"]), BLOCKS + ("vol",))
    placed = (P("vol", BLOCKS, None), P("vol", BLOCKS), P("vol", BLOCKS, None), P(), P())
    return jax.shard_map(
        shards,
        mesh=fine,
        in_specs=placed,
        out_specs=(P("vol", BLOCKS, None), P(), P()),
        check_vma=False,
    )
```

```python
import functools
import itertools
import math

import jax
import jax.numpy as jnp
from jax import lax
from jax.experimental import pallas as pl
from jax.experimental.pallas import tpu as pltpu
from jax.sharding import Mesh
from jax.sharding import PartitionSpec as P

BLOCKS = ("z", "x", "core")
NEAR = ("x", "core", "vol")
F32 = jnp.float32
BF16 = jnp.bfloat16

ROW = 256
WIDE = 384
GRADS = 384
SENT = BF16


def iota(shape, dim):
    return lax.broadcasted_iota(jnp.int32, shape, dim)


def live_rows(active_ref):
    slot = iota((8, ROW), 0)
    out = jnp.zeros((8, ROW), F32)
    for b in range(8):
        out = jnp.where(slot == b, active_ref[0, b].astype(F32), out)
    return out


def repeat_lanes(rows, lanes):
    return (iota((rows, lanes), 1) % rows == iota((rows, lanes), 0)).astype(BF16)


def widen(row, halves):
    slot, lane = iota((8, 128), 0), iota((8, 128), 1)
    first, second = row[:, :128], row[:, 128:]
    right = pltpu.roll(first, 7, 0)
    left = pltpu.roll(second, 1, 0)
    edge = jnp.where(
        (slot % 2 == 0) & (lane < 32), right, jnp.where((slot % 2 == 1) & (lane >= 96), left, 0.0)
    )
    parts = [first, second, edge]
    if halves:
        parts += [jnp.where(lane >= 96, edge, second), jnp.where(lane < 32, edge, first)]
    return jnp.concatenate(parts, axis=1)


def put_plane(outer, inner, z, rows, halves=True):
    full = [widen(row, halves) for row in rows]
    upper = (iota(full[0].shape, 0) // 2) % 2
    low = jnp.where(upper == 1, pltpu.roll(full[7], 2, 0), 0.0)
    high = jnp.where(upper == 0, pltpu.roll(full[0], 6, 0), 0.0)
    ring = [low] + full + [high]
    for k in range(5):
        outer[z, 16 * k : 16 * k + 16] = jnp.concatenate(ring[2 * k : 2 * k + 2], 0).astype(BF16)
    for k in range(4):
        inner[z, 16 * k : 16 * k + 16] = jnp.concatenate(full[2 * k : 2 * k + 2], 0).astype(BF16)


def window(outer, inner, first, count, oz, oy, lanes):
    source = inner if oy == 1 else outer
    start = 16 if oy == 2 else 0
    rows = source[first + oz : first + oz + count, start : start + 64, lanes]
    return rows.reshape(count * 64, rows.shape[-1])


def convolve(outer, inner, bands, first, count):
    left = [
        window(outer, inner, first, count, index // 3, index % 3, slice(0, WIDE)) for index in range(9)
    ]
    return jnp.dot(
        jnp.concatenate(left, 1), bands[...].reshape(9 * WIDE, ROW), preferred_element_type=F32
    )


def slopes(pre, dy, fine):
    sig = 0.5 * jnp.tanh(0.5 * pre) + 0.5
    silu = pre * sig
    return (dy * sig * (1.0 + (pre - silu))).astype(BF16), fine + silu


def put_state(state, z, rows):
    for qy in range(2):
        for half in range(2):
            pair = [rows[2 * half + k][8 * qy : 8 * qy + 8] for k in range(2)]
            start = 32 * (z // 2) + 16 * half
            state[2 * (z % 2) + qy, start : start + 16] = jnp.concatenate(pair, 0).astype(BF16)


def put_bands(bands, index, taps):
    spot = iota((32, ROW), 1) // 32
    for i in range(8):
        part = jnp.zeros((32, ROW), F32)
        for ox in range(3):
            part = jnp.where(spot == i + 1 - ox, taps[ox], part)
        bands[index, 32 * i : 32 * i + 32] = part.astype(BF16)
    bands[index, 256:288] = jnp.where(spot == 7, taps[2], 0.0).astype(BF16)
    bands[index, 288:352] = jnp.zeros((64, ROW), BF16)
    bands[index, 352:384] = jnp.where(spot == 0, taps[0], 0.0).astype(BF16)


def pack_kernel(
    active, features, coarse, conv, down, to_core, to_chip, coarse_rows, live_out, fine_out, conv_out, down_out,
    flags, flat, sems,
):
    ends = [slice(0, 4096), slice(12288, 16384), slice(4096, 12288)]
    copies = [
        pltpu.make_async_copy(active, flags, sems.at[0]),
        pltpu.make_async_copy(coarse, flat, sems.at[1]),
    ]
    copies += [
        pltpu.make_async_copy(features.at[:, lanes], fine_out.at[:, lanes], sems.at[2 + k])
        for k, lanes in enumerate(ends)
    ]
    copies += [
        pltpu.make_async_copy(conv, conv_out, sems.at[5]),
        pltpu.make_async_copy(down, down_out, sems.at[6]),
    ]
    for copy in copies:
        copy.start()
    copies[0].wait()
    live = live_rows(flags)
    live_out[...] = live
    slot = iota((8, ROW), 0)
    copies[1].wait()

    def coarse_row(zc, yc):
        parts = []
        for b in range(8):
            start = ((((b // 4) * 4 + zc) * 8 + ((b // 2) % 2) * 4 + yc) * 2 + b % 2) * ROW
            parts.append(flat[:, start : start + ROW].astype(F32))
        return jnp.concatenate(parts, 0) * live

    ends = {}
    for zc in range(4):
        for half in range(2):
            both = [coarse_row(zc, 2 * half + k) for k in range(2)]
            start = 32 * zc + 16 * half
            coarse_rows[start : start + 16] = jnp.concatenate(both, 0).astype(BF16)
            ends[zc, half] = both
    second = lax.axis_index("core") == 1

    def send(start, to_next, to_prev):
        to_core[:, start : start + ROW] = jnp.where(second, to_prev, to_next).astype(BF16)
        to_chip[:, start : start + ROW] = jnp.where(second, to_next, to_prev).astype(BF16)

    for half in range(2):
        last, first = ends[3, half], ends[0, half]
        send(
            2048 + half * ROW,
            jnp.where(slot < 4, pltpu.roll(last[0], 4, 0), last[1]),
            jnp.where(slot < 4, first[1], pltpu.roll(first[0], 4, 0)),
        )

    def fine(z, y):
        start = (z * 8 + y) * ROW
        return fine_out[:, start : start + ROW].astype(F32) * live

    copies[2].wait()
    copies[3].wait()
    for y in range(8):
        send(
            y * ROW,
            jnp.where(slot < 4, pltpu.roll(fine(6, y), 4, 0), fine(7, y)),
            jnp.where(slot < 4, fine(1, y), pltpu.roll(fine(0, y), 4, 0)),
        )
    for copy in copies[4:]:
        copy.wait()


def inner_kernel(
    live_in, features, conv, down, coarse, outer, inner, bands, spread, dpre, dy, state, pre, spread_out,
):
    live = live_in[...]
    tile = repeat_lanes(32, ROW)
    spot = iota((64, ROW), 1) // 32
    for q in range(4):
        turned = [
            lax.dot_general(down[2 * q + ox], tile, (((0,), (0,)), ((), ())), preferred_element_type=F32)
            for ox in range(2)
        ]
        for cx in range(4):
            part = jnp.where(spot == 2 * cx, turned[0], jnp.where(spot == 2 * cx + 1, turned[1], 0.0))
            spread[64 * cx : 64 * cx + 64, ROW * q : ROW * q + ROW] = part.astype(BF16)
    spread_out[...] = jnp.dot(coarse[...], spread[...], preferred_element_type=F32)
    taps = jnp.dot(conv[...].reshape(27 * 32, 32), tile, preferred_element_type=F32)
    for index in range(9):
        put_bands(bands, index, [taps[96 * index + 32 * ox : 96 * index + 32 * ox + 32] for ox in range(3)])
    for z in range(8):
        rows = []
        for y in range(8):
            start = (z * 8 + y) * ROW
            rows.append(features[:, start : start + ROW].astype(F32) * live)
        put_plane(outer, inner, z, rows)
    for z in range(0, 6, 2):
        pre[64 * z : 64 * z + 128] = convolve(outer, inner, bands, z, 2)
    for z in range(8):
        qz, rows = z % 2, []
        for pair in range(4):
            part = slice(16 * pair, 16 * pair + 16)
            base = 32 * (z // 2) + 8 * pair
            lanes = [slice(ROW * (2 * qz + qy), ROW * (2 * qz + qy) + ROW) for qy in range(2)]
            spread_rows = jnp.concatenate([spread_out[base : base + 8, lane] for lane in lanes], 0)
            dy[z, part] = spread_rows
            if 1 <= z <= 6:
                start = 64 * (z - 1) + 16 * pair
                fine = inner[z, part, :ROW].astype(F32)
                dpre[z - 1, part], y = slopes(pre[start : start + 16], spread_rows, fine)
                rows.append(y)
        if rows:
            put_state(state, z, rows)
    for z in (0, 7):
        put_state(state, z, [jnp.zeros((16, ROW), F32)] * 4)


def main_kernel(
    scale, inner_own, outer_own, from_chip, from_core, coarse, bands, spread, dpre_own, dy, state_own,
    grads, dpre, outer, inner, ends, pre, state,
):
    slot = iota((8, ROW), 0)
    outer[2:10] = outer_own[...]
    inner[2:10] = inner_own[...]
    dpre[2:8] = dpre_own[...]
    state[...] = state_own[...]

    second = lax.axis_index("core") == 1

    def received(start):
        core = from_core[:, start : start + ROW].astype(F32)
        chip = from_chip[:, start : start + ROW].astype(F32)
        return jnp.where(second, core, chip), jnp.where(second, chip, core)

    def own(z, y):
        return inner_own[z, 16 * (y // 2) : 16 * (y // 2) + 16, :ROW].astype(F32)[8 * (y % 2) : 8 * (y % 2) + 8]

    before, beyond, after, past = [], [], [], []
    for y in range(8):
        low, high = received(y * ROW)
        beyond.append(jnp.where(slot < 4, low, pltpu.roll(own(6, y), 4, 0)))
        before.append(pltpu.roll(jnp.where(slot >= 4, low, own(7, y)), 4, 0))
        after.append(jnp.where(slot >= 4, high, pltpu.roll(own(0, y), 4, 0)))
        past.append(pltpu.roll(jnp.where(slot < 4, high, own(1, y)), 4, 0))
    for z, rows in ((0, beyond), (1, before), (10, after), (11, past)):
        put_plane(outer, inner, z, rows)

    for k in range(2):
        low, high = received(2048 + k * ROW)
        last = coarse[96 + 16 * k : 112 + 16 * k].astype(F32)
        first = coarse[16 * k : 16 * k + 16].astype(F32)
        under = [
            jnp.where(slot < 4, low, pltpu.roll(last[:8], 4, 0)),
            pltpu.roll(jnp.where(slot >= 4, low, last[8:]), 4, 0),
        ]
        over = [
            jnp.where(slot >= 4, high, pltpu.roll(first[:8], 4, 0)),
            pltpu.roll(jnp.where(slot < 4, high, first[8:]), 4, 0),
        ]
        ends[0, 16 * k : 16 * k + 16] = jnp.concatenate(under, 0).astype(BF16)
        ends[1, 16 * k : 16 * k + 16] = jnp.concatenate(over, 0).astype(BF16)
    dy_end = [
        jnp.dot(ends[0], spread[:, 2 * ROW :], preferred_element_type=F32),
        jnp.dot(ends[1], spread[:, : 2 * ROW], preferred_element_type=F32),
    ]

    for side in range(2):
        pre[side] = convolve(outer, inner, bands, 8 * side, 2)
    for side in range(2):
        for k in range(2):
            step = 8 * side + k
            z = step - 1
            rows = []
            for pair in range(4):
                part = slice(16 * pair, 16 * pair + 16)
                if 0 <= z < 8:
                    back = dy[z, part]
                else:
                    back = jnp.concatenate(
                        [dy_end[side][8 * pair : 8 * pair + 8, ROW * qy : ROW * qy + ROW] for qy in range(2)], 0
                    )
                start = 64 * k + 16 * pair
                fine = inner[step + 1, part, :ROW].astype(F32)
                dpre[step, part], y = slopes(pre[side, start : start + 16], back, fine)
                rows.append(y)
            if 0 <= z < 8:
                put_state(state, z, rows)

    lane = iota((32, 128), 1)
    v0, v1, low1, high1 = slice(0, 128), slice(128, 256), slice(384, 512), slice(512, 640)
    turned = dpre[1:9].reshape(512, ROW).T
    turned = jnp.concatenate([turned[:128], turned[128:]], 1)
    blocks = []
    for oz in range(3):
        right = []
        for oy in range(3):
            halves = [
                jnp.concatenate([window(outer, inner, 1, 8, oz, oy, part) for part in parts], 1)
                for parts in ((v0, low1), (v1, high1))
            ]
            right.append(jnp.concatenate(halves, 0))
        products = jnp.dot(turned, jnp.concatenate(right, 1), preferred_element_type=F32)
        for oy in range(3):
            block = [products[32 * j : 32 * j + 32, ROW * oy : ROW * oy + ROW] for j in range(4)]
            t0 = jnp.where(lane >= 96, block[0][:, v1], block[0][:, v0])
            t3 = jnp.where(lane < 32, block[3][:, v1], block[3][:, v0])
            folded = (
                pltpu.roll(t0, 32, 1)
                + block[1][:, v0]
                + pltpu.roll(block[2][:, v0], 96, 1)
                + pltpu.roll(t3, 64, 1)
            )
            blocks.append(jnp.where(lane < 96, folded * scale, 0.0))
    for index in range(8):
        both = blocks[index]
        if index < 3:
            both = jnp.where(lane < 96, both, pltpu.roll(blocks[8], 96 - 32 * index, 1))
        grads[32 * index : 32 * index + 32] = both.astype(SENT)
    left = jnp.concatenate(
        [jnp.concatenate([state[q][:, v0], state[q][:, v1]], 0) for q in range(4)], 1
    )
    right = jnp.concatenate([coarse[:, v0], coarse[:, v1]], 0)
    products = lax.dot_general(left, right, (((0,), (0,)), ((), ())), preferred_element_type=F32)
    for q in range(4):
        block = [products[128 * q + 32 * x : 128 * q + 32 * x + 32] for x in range(4)]
        folded = jnp.where(lane < 64, block[0], block[3]) + pltpu.roll(
            jnp.where(lane < 64, block[1], block[2]), 64, 1
        )
        grads[256 + 32 * q : 288 + 32 * q] = (folded * scale).astype(SENT)


def back_kernel(live_in, conv, dpre, dy, result, outer, inner, bands):
    live = live_in[...]
    tile = repeat_lanes(32, ROW)
    for index in range(9):
        taps = [
            lax.dot_general(
                conv[26 - (3 * index + ox)], tile, (((0,), (0,)), ((), ())), preferred_element_type=F32
            )
            for ox in range(3)
        ]
        put_bands(bands, index, taps)
    for z in range(10):
        rows = []
        for pair in range(4):
            both = dpre[z, 16 * pair : 16 * pair + 16].astype(F32)
            rows += [both[:8], both[8:]]
        put_plane(outer, inner, z, rows, halves=False)
    total = convolve(outer, inner, bands, 0, 8)
    for z in range(8):
        for y in range(8):
            row = 64 * z + 8 * y
            value = dy[z, 8 * y : 8 * y + 8] + live * total[row : row + 8]
            result[:, row * 32 : row * 32 + ROW] = value.astype(BF16)


def back_turn(turn, *refs):
    *arrays, out, result, outer, inner, bands, sem = refs
    first = lax.axis_index("z") * 8 < 3 * lax.axis_size("z")

    @pl.when(first if turn == 0 else jnp.logical_not(first))
    def _():
        back_kernel(*arrays[turn:], result, outer, inner, bands)
        copy = pltpu.make_async_copy(result, out, sem.at[0])
        copy.start()
        copy.wait()


def sum_kernel(piece, parts, out):
    unit = math.lcm(piece, 16)
    total = parts[:unit].astype(F32)
    for start in range(unit, parts.shape[0], unit):
        total = total + parts[start : start + unit].astype(F32)
    pieces = [total[start : start + piece] for start in range(0, unit, piece)]
    total = sum(pieces[1:], pieces[0])
    whole = jnp.concatenate([total] * len(pieces), 0).astype(out.dtype)
    for start in range(0, out.shape[0], unit):
        out[start : start + unit] = whole


def finish_kernel(whole, conv_grad, down_grad):
    for index in range(8):
        turned = whole[32 * index : 32 * index + 32].astype(F32).T
        for ox in range(3):
            conv_grad[3 * index + ox] = turned[32 * ox : 32 * ox + 32]
        if index < 3:
            conv_grad[24 + index] = turned[96:]
    for q in range(4):
        both = whole[256 + 32 * q : 288 + 32 * q].astype(F32)
        down_grad[2 * q] = both[:, :64]
        down_grad[2 * q + 1] = pltpu.roll(both, 64, 1)[:, :64]


def exchange(rows, axes, groups=None):
    cut = rows.reshape(lax.axis_size(axes), -1, 4, 128)
    return lax.all_to_all(cut, axes, 0, 0, axis_index_groups=groups).reshape(rows.shape)


def call(kernel, outs, arrays, scratch=(), far=0, out_space=pltpu.VMEM, same=(), name=None):
    arrays = [pltpu.with_memory_space_constraint(a, pltpu.HBM) for a in arrays[:far]] + arrays[far:]
    spaces = [pltpu.HBM] * far + [pltpu.VMEM] * (len(arrays) - far)
    return pl.pallas_call(
        kernel,
        out_shape=[jax.ShapeDtypeStruct(shape, dtype) for shape, dtype in outs],
        in_specs=[pl.BlockSpec(memory_space=space) for space in spaces],
        out_specs=[pl.BlockSpec(memory_space=out_space)] * len(outs),
        input_output_aliases=dict(same),
        scratch_shapes=scratch,
        compiler_params=pltpu.CompilerParams(vmem_limit_bytes=40 * 2**20),
        name=name,
    )(*arrays)


def plane_order():
    sizes = [lax.axis_size(axis) for axis in NEAR]
    shift = [sizes[0] // 2, 1, sizes[2] // 2]
    spots = itertools.product(*[range(size) for size in sizes])
    return [
        ((x + shift[0]) % sizes[0] * sizes[1] + (core + shift[1]) % sizes[1]) * sizes[2]
        + (vol + shift[2]) % sizes[2]
        for x, core, vol in spots
    ]


def shards(features, active, coarse_grad, conv_weight, down_weight):
    fine = features[0]
    devices = lax.axis_size(BLOCKS)
    scale = (lax.axis_size("vol") * devices * fine.size // 32) ** -0.5
    full = WIDE + ROW
    to_core, to_chip, coarse, live, fine, conv, down = call(
        pack_kernel,
        [
            ((8, 2560), BF16), ((8, 2560), BF16), ((128, ROW), BF16), ((8, ROW), F32),
            (fine.shape, BF16), (conv_weight.shape, BF16), (down_weight.shape, BF16),
        ],
        [active, fine, coarse_grad[0], conv_weight, down_weight],
        [
            pltpu.SMEM(active.shape, jnp.int32),
            pltpu.VMEM(coarse_grad.shape[1:], BF16),
            pltpu.SemaphoreType.DMA((7,)),
        ],
        far=5, name="pack",
    )
    pairs = [(i, i + 1) for i in range(1, devices - 1, 2)]
    from_chip = lax.ppermute(to_chip, BLOCKS, pairs + [(j, i) for i, j in pairs])
    from_core = lax.ppermute(to_core, "core", [(0, 1), (1, 0)])
    outer, inner, bands, spread, dpre, dy, state = call(
        inner_kernel,
        [
            ((8, 80, full), BF16), ((8, 64, full), BF16), ((9, WIDE, ROW), BF16), ((ROW, 4 * ROW), BF16),
            ((6, 64, ROW), BF16), ((8, 64, ROW), F32), ((4, 128, ROW), BF16),
        ],
        [live, fine, conv, down, coarse],
        [pltpu.VMEM((384, ROW), F32), pltpu.VMEM((128, 4 * ROW), F32)],
        name="inner",
    )
    grads, dpre = call(
        lambda *refs: main_kernel(scale, *refs),
        [((GRADS, 128), SENT), ((10, 64, ROW), BF16)],
        [inner, outer, from_chip, from_core, coarse, bands, spread, dpre, dy, state],
        [
            pltpu.VMEM((12, 80, full), BF16), pltpu.VMEM((12, 64, full), BF16), pltpu.VMEM((2, 32, ROW), BF16),
            pltpu.VMEM((2, 128, ROW), F32), pltpu.VMEM((4, 128, ROW), BF16),
        ],
        name="main",
    )
    near, far = lax.axis_size(NEAR), lax.axis_size("z")
    plane = plane_order()
    add = functools.partial(sum_kernel, GRADS // near)
    parts = exchange(grads, NEAR, [plane])
    def back(turn, arrays):
        (result,) = call(
            functools.partial(back_turn, turn), [((8, 64 * ROW), BF16)], arrays + [live, conv, dpre, dy],
            [
                pltpu.VMEM((8, 64 * ROW), BF16), pltpu.VMEM((10, 80, WIDE), BF16),
                pltpu.VMEM((10, 64, WIDE), BF16), pltpu.VMEM((9, WIDE, ROW), BF16),
                pltpu.SemaphoreType.DMA((1,)),
            ],
            far=turn, out_space=pltpu.HBM, same=[(0, 0)] * turn, name=f"back{turn}",
        )
        return result

    parts, dpre = lax.optimization_barrier((parts, dpre))
    result = back(0, [])
    (sums,) = call(add, [((far * GRADS // near, 128), SENT)], [parts], name="sum_near")
    sums, result = lax.optimization_barrier((sums, result))
    sums = exchange(sums, "z", [[(k + far // 2) % far for k in range(far)]])
    (sums,) = call(add, [((GRADS, 128), SENT)], [sums], name="sum_far")
    whole, result = lax.optimization_barrier((exchange(sums, NEAR, [plane]), result))
    conv_grad, down_grad = call(
        finish_kernel, [((27, 32, 32), F32), ((8, 32, 64), F32)], [whole], name="finish"
    )
    result = back(1, [result])
    return result[None], conv_grad, down_grad


def solution(mesh):
    fine = Mesh(mesh.devices.reshape(-1, 4, 2, mesh.shape["vol"]), BLOCKS + ("vol",))
    placed = (P("vol", BLOCKS, None), P("vol", BLOCKS), P("vol", BLOCKS, None), P(), P())
    return jax.shard_map(
        shards,
        mesh=fine,
        in_specs=placed,
        out_specs=(P("vol", BLOCKS, None), P(), P()),
        check_vma=False,
    )
```

```python
import functools
import itertools
import math

import jax
import jax.numpy as jnp
from jax import lax
from jax.experimental import pallas as pl
from jax.experimental.pallas import tpu as pltpu
from jax.sharding import Mesh
from jax.sharding import PartitionSpec as P

BLOCKS = ("z", "x", "core")
NEAR = ("x", "core", "vol")
F32 = jnp.float32
BF16 = jnp.bfloat16

ROW = 256
WIDE = 384
TAPS = 1024
GRADS = 384
SENT = BF16


def iota(shape, dim):
    return lax.broadcasted_iota(jnp.int32, shape, dim)


def live_rows(active_ref):
    slot = iota((8, ROW), 0)
    out = jnp.zeros((8, ROW), F32)
    for b in range(8):
        out = jnp.where(slot == b, active_ref[0, b].astype(F32), out)
    return out


def repeat_lanes(rows, lanes):
    return (iota((rows, lanes), 1) % rows == iota((rows, lanes), 0)).astype(BF16)


def widen(row, halves):
    slot, lane = iota((8, 128), 0), iota((8, 128), 1)
    first, second = row[:, :128], row[:, 128:]
    right = pltpu.roll(first, 7, 0)
    left = pltpu.roll(second, 1, 0)
    edge = jnp.where(
        (slot % 2 == 0) & (lane < 32), right, jnp.where((slot % 2 == 1) & (lane >= 96), left, 0.0)
    )
    parts = [first, second, edge]
    if halves:
        parts += [jnp.where(lane >= 96, edge, second), jnp.where(lane < 32, edge, first)]
    return jnp.concatenate(parts, axis=1)


def put_plane(outer, inner, z, rows, halves=True):
    full = [widen(row, halves) for row in rows]
    upper = (iota(full[0].shape, 0) // 2) % 2
    low = jnp.where(upper == 1, pltpu.roll(full[7], 2, 0), 0.0)
    high = jnp.where(upper == 0, pltpu.roll(full[0], 6, 0), 0.0)
    ring = [low] + full + [high]
    for k in range(5):
        outer[z, 16 * k : 16 * k + 16] = jnp.concatenate(ring[2 * k : 2 * k + 2], 0).astype(BF16)
    tile = slice(ROW, WIDE)
    edges = [ring[y][:, tile] + pltpu.roll(ring[y + 1][:, tile], 64, 1) for y in range(8)]
    both = [jnp.concatenate([row[:, :ROW], edge, row[:, WIDE:]], 1) if halves
            else jnp.concatenate([row[:, :ROW], edge], 1) for row, edge in zip(full, edges)]
    for k in range(4):
        inner[z, 16 * k : 16 * k + 16] = jnp.concatenate(both[2 * k : 2 * k + 2], 0).astype(BF16)


def window(outer, inner, first, count, oz, oy, lanes):
    source = inner if oy == 1 else outer
    start = 16 if oy == 2 else 0
    rows = source[first + oz : first + oz + count, start : start + 64, lanes]
    return rows.reshape(count * 64, rows.shape[-1])


def convolve(outer, inner, bands, first, count):
    left = [
        window(outer, inner, first, count, index // 3, index % 3, slice(0, WIDE if index % 3 else ROW))
        for index in range(9)
    ]
    return jnp.dot(
        jnp.concatenate(left, 1), bands[...].reshape(3 * TAPS, ROW), preferred_element_type=F32
    )


def slopes(pre, dy, fine):
    sig = 0.5 * jnp.tanh(0.5 * pre) + 0.5
    silu = pre * sig
    return (dy * sig * (1.0 + (pre - silu))).astype(BF16), fine + silu


def put_state(state, z, rows):
    for qy in range(2):
        for half in range(2):
            pair = [rows[2 * half + k][8 * qy : 8 * qy + 8] for k in range(2)]
            start = 32 * (z // 2) + 16 * half
            state[2 * (z % 2) + qy, start : start + 16] = jnp.concatenate(pair, 0).astype(BF16)


def put_bands(bands, index, taps):
    spot = iota((32, ROW), 1) // 32
    oz, oy = index // 3, index % 3
    start = (0, ROW, ROW + WIDE)[oy]
    for i in range(8):
        part = jnp.zeros((32, ROW), F32)
        for ox in range(3):
            part = jnp.where(spot == i + 1 - ox, taps[ox], part)
        bands[oz, start + 32 * i : start + 32 * i + 32] = part.astype(BF16)
    edge = 2 * ROW if oy < 2 else TAPS - 128
    right, left = (64, 32) if oy == 1 else (0, 96)
    bands[oz, edge + right : edge + right + 32] = jnp.where(spot == 7, taps[2], 0.0).astype(BF16)
    bands[oz, edge + left : edge + left + 32] = jnp.where(spot == 0, taps[0], 0.0).astype(BF16)
    if oy == 2:
        bands[oz, edge + 32 : edge + 96] = jnp.zeros((64, ROW), BF16)


def pack_kernel(
    active, features, coarse, conv, down, to_core, to_chip, coarse_rows, live_out, fine_out, conv_out, down_out,
    flags, flat, sems,
):
    ends = [slice(0, 4096), slice(12288, 16384), slice(4096, 12288)]
    copies = [
        pltpu.make_async_copy(active, flags, sems.at[0]),
        pltpu.make_async_copy(coarse, flat, sems.at[1]),
    ]
    copies += [
        pltpu.make_async_copy(features.at[:, lanes], fine_out.at[:, lanes], sems.at[2 + k])
        for k, lanes in enumerate(ends)
    ]
    copies += [
        pltpu.make_async_copy(conv, conv_out, sems.at[5]),
        pltpu.make_async_copy(down, down_out, sems.at[6]),
    ]
    for copy in copies:
        copy.start()
    copies[0].wait()
    live = live_rows(flags)
    live_out[...] = live
    slot = iota((8, ROW), 0)
    copies[1].wait()

    def coarse_row(zc, yc):
        parts = []
        for b in range(8):
            start = ((((b // 4) * 4 + zc) * 8 + ((b // 2) % 2) * 4 + yc) * 2 + b % 2) * ROW
            parts.append(flat[:, start : start + ROW].astype(F32))
        return jnp.concatenate(parts, 0) * live

    ends = {}
    for zc in range(4):
        for half in range(2):
            both = [coarse_row(zc, 2 * half + k) for k in range(2)]
            start = 32 * zc + 16 * half
            coarse_rows[start : start + 16] = jnp.concatenate(both, 0).astype(BF16)
            ends[zc, half] = both
    second = lax.axis_index("core") == 1

    def send(start, to_next, to_prev):
        to_core[:, start : start + ROW] = jnp.where(second, to_prev, to_next).astype(BF16)
        to_chip[:, start : start + ROW] = jnp.where(second, to_next, to_prev).astype(BF16)

    for half in range(2):
        last, first = ends[3, half], ends[0, half]
        send(
            2048 + half * ROW,
            jnp.where(slot < 4, pltpu.roll(last[0], 4, 0), last[1]),
            jnp.where(slot < 4, first[1], pltpu.roll(first[0], 4, 0)),
        )

    def fine(z, y):
        start = (z * 8 + y) * ROW
        return fine_out[:, start : start + ROW].astype(F32) * live

    copies[2].wait()
    copies[3].wait()
    for y in range(8):
        send(
            y * ROW,
            jnp.where(slot < 4, pltpu.roll(fine(6, y), 4, 0), fine(7, y)),
            jnp.where(slot < 4, fine(1, y), pltpu.roll(fine(0, y), 4, 0)),
        )
    for copy in copies[4:]:
        copy.wait()


def inner_kernel(
    live_in, features, conv, down, coarse, outer, inner, bands, spread, dpre, dy, state, pre, spread_out,
):
    live = live_in[...]
    tile = repeat_lanes(32, ROW)
    spot = iota((64, ROW), 1) // 32
    for q in range(4):
        turned = [
            lax.dot_general(down[2 * q + ox], tile, (((0,), (0,)), ((), ())), preferred_element_type=F32)
            for ox in range(2)
        ]
        for cx in range(4):
            part = jnp.where(spot == 2 * cx, turned[0], jnp.where(spot == 2 * cx + 1, turned[1], 0.0))
            spread[64 * cx : 64 * cx + 64, ROW * q : ROW * q + ROW] = part.astype(BF16)
    spread_out[...] = jnp.dot(coarse[...], spread[...], preferred_element_type=F32)
    taps = jnp.dot(conv[...].reshape(27 * 32, 32), tile, preferred_element_type=F32)
    for index in range(9):
        put_bands(bands, index, [taps[96 * index + 32 * ox : 96 * index + 32 * ox + 32] for ox in range(3)])
    for z in range(8):
        rows = []
        for y in range(8):
            start = (z * 8 + y) * ROW
            rows.append(features[:, start : start + ROW].astype(F32) * live)
        put_plane(outer, inner, z, rows)
    for z in range(0, 6, 2):
        pre[64 * z : 64 * z + 128] = convolve(outer, inner, bands, z, 2)
    for z in range(8):
        qz, rows = z % 2, []
        for pair in range(4):
            part = slice(16 * pair, 16 * pair + 16)
            base = 32 * (z // 2) + 8 * pair
            lanes = [slice(ROW * (2 * qz + qy), ROW * (2 * qz + qy) + ROW) for qy in range(2)]
            spread_rows = jnp.concatenate([spread_out[base : base + 8, lane] for lane in lanes], 0)
            dy[z, part] = spread_rows
            if 1 <= z <= 6:
                start = 64 * (z - 1) + 16 * pair
                fine = inner[z, part, :ROW].astype(F32)
                dpre[z - 1, part], y = slopes(pre[start : start + 16], spread_rows, fine)
                rows.append(y)
        if rows:
            put_state(state, z, rows)
    for z in (0, 7):
        put_state(state, z, [jnp.zeros((16, ROW), F32)] * 4)


def main_kernel(
    scale, inner_own, outer_own, from_chip, from_core, coarse, bands, spread, dpre_own, dy, state_own,
    grads, dpre, outer, inner, ends, pre, state,
):
    slot = iota((8, ROW), 0)
    outer[2:10] = outer_own[...]
    inner[2:10] = inner_own[...]
    dpre[2:8] = dpre_own[...]
    state[...] = state_own[...]

    second = lax.axis_index("core") == 1

    def received(start):
        core = from_core[:, start : start + ROW].astype(F32)
        chip = from_chip[:, start : start + ROW].astype(F32)
        return jnp.where(second, core, chip), jnp.where(second, chip, core)

    def own(z, y):
        return inner_own[z, 16 * (y // 2) : 16 * (y // 2) + 16, :ROW].astype(F32)[8 * (y % 2) : 8 * (y % 2) + 8]

    before, beyond, after, past = [], [], [], []
    for y in range(8):
        low, high = received(y * ROW)
        beyond.append(jnp.where(slot < 4, low, pltpu.roll(own(6, y), 4, 0)))
        before.append(pltpu.roll(jnp.where(slot >= 4, low, own(7, y)), 4, 0))
        after.append(jnp.where(slot >= 4, high, pltpu.roll(own(0, y), 4, 0)))
        past.append(pltpu.roll(jnp.where(slot < 4, high, own(1, y)), 4, 0))
    for z, rows in ((0, beyond), (1, before), (10, after), (11, past)):
        put_plane(outer, inner, z, rows)

    for k in range(2):
        low, high = received(2048 + k * ROW)
        last = coarse[96 + 16 * k : 112 + 16 * k].astype(F32)
        first = coarse[16 * k : 16 * k + 16].astype(F32)
        under = [
            jnp.where(slot < 4, low, pltpu.roll(last[:8], 4, 0)),
            pltpu.roll(jnp.where(slot >= 4, low, last[8:]), 4, 0),
        ]
        over = [
            jnp.where(slot >= 4, high, pltpu.roll(first[:8], 4, 0)),
            pltpu.roll(jnp.where(slot < 4, high, first[8:]), 4, 0),
        ]
        ends[0, 16 * k : 16 * k + 16] = jnp.concatenate(under, 0).astype(BF16)
        ends[1, 16 * k : 16 * k + 16] = jnp.concatenate(over, 0).astype(BF16)
    dy_end = [
        jnp.dot(ends[0], spread[:, 2 * ROW :], preferred_element_type=F32),
        jnp.dot(ends[1], spread[:, : 2 * ROW], preferred_element_type=F32),
    ]

    for side in range(2):
        pre[side] = convolve(outer, inner, bands, 8 * side, 2)
    for side in range(2):
        for k in range(2):
            step = 8 * side + k
            z = step - 1
            rows = []
            for pair in range(4):
                part = slice(16 * pair, 16 * pair + 16)
                if 0 <= z < 8:
                    back = dy[z, part]
                else:
                    back = jnp.concatenate(
                        [dy_end[side][8 * pair : 8 * pair + 8, ROW * qy : ROW * qy + ROW] for qy in range(2)], 0
                    )
                start = 64 * k + 16 * pair
                fine = inner[step + 1, part, :ROW].astype(F32)
                dpre[step, part], y = slopes(pre[side, start : start + 16], back, fine)
                rows.append(y)
            if 0 <= z < 8:
                put_state(state, z, rows)

    lane = iota((32, 128), 1)
    v0, v1, low1, high1 = slice(0, 128), slice(128, 256), slice(384, 512), slice(512, 640)
    turned = dpre[1:9].reshape(512, ROW).T
    turned = jnp.concatenate([turned[:128], turned[128:]], 1)
    blocks = []
    for oz in range(3):
        right = []
        for oy in range(3):
            halves = [
                jnp.concatenate([window(outer, inner, 1, 8, oz, oy, part) for part in parts], 1)
                for parts in ((v0, low1), (v1, high1))
            ]
            right.append(jnp.concatenate(halves, 0))
        products = jnp.dot(turned, jnp.concatenate(right, 1), preferred_element_type=F32)
        for oy in range(3):
            block = [products[32 * j : 32 * j + 32, ROW * oy : ROW * oy + ROW] for j in range(4)]
            t0 = jnp.where(lane >= 96, block[0][:, v1], block[0][:, v0])
            t3 = jnp.where(lane < 32, block[3][:, v1], block[3][:, v0])
            folded = (
                pltpu.roll(t0, 32, 1)
                + block[1][:, v0]
                + pltpu.roll(block[2][:, v0], 96, 1)
                + pltpu.roll(t3, 64, 1)
            )
            blocks.append(jnp.where(lane < 96, folded * scale, 0.0))
    for index in range(8):
        both = blocks[index]
        if index < 3:
            both = jnp.where(lane < 96, both, pltpu.roll(blocks[8], 96 - 32 * index, 1))
        grads[32 * index : 32 * index + 32] = both.astype(SENT)
    left = jnp.concatenate(
        [jnp.concatenate([state[q][:, v0], state[q][:, v1]], 0) for q in range(4)], 1
    )
    right = jnp.concatenate([coarse[:, v0], coarse[:, v1]], 0)
    products = lax.dot_general(left, right, (((0,), (0,)), ((), ())), preferred_element_type=F32)
    for q in range(4):
        block = [products[128 * q + 32 * x : 128 * q + 32 * x + 32] for x in range(4)]
        folded = jnp.where(lane < 64, block[0], block[3]) + pltpu.roll(
            jnp.where(lane < 64, block[1], block[2]), 64, 1
        )
        grads[256 + 32 * q : 288 + 32 * q] = (folded * scale).astype(SENT)


def back_kernel(live_in, conv, dpre, dy, result, outer, inner, bands):
    live = live_in[...]
    tile = repeat_lanes(32, ROW)
    for index in range(9):
        taps = [
            lax.dot_general(
                conv[26 - (3 * index + ox)], tile, (((0,), (0,)), ((), ())), preferred_element_type=F32
            )
            for ox in range(3)
        ]
        put_bands(bands, index, taps)
    for z in range(10):
        rows = []
        for pair in range(4):
            both = dpre[z, 16 * pair : 16 * pair + 16].astype(F32)
            rows += [both[:8], both[8:]]
        put_plane(outer, inner, z, rows, halves=False)
    total = convolve(outer, inner, bands, 0, 8)
    for z in range(8):
        for y in range(8):
            row = 64 * z + 8 * y
            value = dy[z, 8 * y : 8 * y + 8] + live * total[row : row + 8]
            result[:, row * 32 : row * 32 + ROW] = value.astype(BF16)


def back_turn(turn, *refs):
    *arrays, out, result, outer, inner, bands, sem = refs
    first = lax.axis_index("z") * 8 < 3 * lax.axis_size("z")

    @pl.when(first if turn == 0 else jnp.logical_not(first))
    def _():
        back_kernel(*arrays[turn:], result, outer, inner, bands)
        copy = pltpu.make_async_copy(result, out, sem.at[0])
        copy.start()
        copy.wait()


def sum_kernel(piece, parts, out):
    unit = math.lcm(piece, 16)
    total = parts[:unit].astype(F32)
    for start in range(unit, parts.shape[0], unit):
        total = total + parts[start : start + unit].astype(F32)
    pieces = [total[start : start + piece] for start in range(0, unit, piece)]
    total = sum(pieces[1:], pieces[0])
    whole = jnp.concatenate([total] * len(pieces), 0).astype(out.dtype)
    for start in range(0, out.shape[0], unit):
        out[start : start + unit] = whole


def finish_kernel(whole, conv_grad, down_grad):
    for index in range(8):
        turned = whole[32 * index : 32 * index + 32].astype(F32).T
        for ox in range(3):
            conv_grad[3 * index + ox] = turned[32 * ox : 32 * ox + 32]
        if index < 3:
            conv_grad[24 + index] = turned[96:]
    for q in range(4):
        both = whole[256 + 32 * q : 288 + 32 * q].astype(F32)
        down_grad[2 * q] = both[:, :64]
        down_grad[2 * q + 1] = pltpu.roll(both, 64, 1)[:, :64]


def exchange(rows, axes, groups=None):
    cut = rows.reshape(lax.axis_size(axes), -1, 4, 128)
    return lax.all_to_all(cut, axes, 0, 0, axis_index_groups=groups).reshape(rows.shape)


def call(kernel, outs, arrays, scratch=(), far=0, out_space=pltpu.VMEM, same=(), name=None):
    arrays = [pltpu.with_memory_space_constraint(a, pltpu.HBM) for a in arrays[:far]] + arrays[far:]
    spaces = [pltpu.HBM] * far + [pltpu.VMEM] * (len(arrays) - far)
    return pl.pallas_call(
        kernel,
        out_shape=[jax.ShapeDtypeStruct(shape, dtype) for shape, dtype in outs],
        in_specs=[pl.BlockSpec(memory_space=space) for space in spaces],
        out_specs=[pl.BlockSpec(memory_space=out_space)] * len(outs),
        input_output_aliases=dict(same),
        scratch_shapes=scratch,
        compiler_params=pltpu.CompilerParams(vmem_limit_bytes=40 * 2**20),
        name=name,
    )(*arrays)


def plane_order():
    sizes = [lax.axis_size(axis) for axis in NEAR]
    shift = [sizes[0] // 2, 1, sizes[2] // 2]
    spots = itertools.product(*[range(size) for size in sizes])
    return [
        ((x + shift[0]) % sizes[0] * sizes[1] + (core + shift[1]) % sizes[1]) * sizes[2]
        + (vol + shift[2]) % sizes[2]
        for x, core, vol in spots
    ]


def shards(features, active, coarse_grad, conv_weight, down_weight):
    fine = features[0]
    devices = lax.axis_size(BLOCKS)
    scale = (lax.axis_size("vol") * devices * fine.size // 32) ** -0.5
    full = WIDE + ROW
    to_core, to_chip, coarse, live, fine, conv, down = call(
        pack_kernel,
        [
            ((8, 2560), BF16), ((8, 2560), BF16), ((128, ROW), BF16), ((8, ROW), F32),
            (fine.shape, BF16), (conv_weight.shape, BF16), (down_weight.shape, BF16),
        ],
        [active, fine, coarse_grad[0], conv_weight, down_weight],
        [
            pltpu.SMEM(active.shape, jnp.int32),
            pltpu.VMEM(coarse_grad.shape[1:], BF16),
            pltpu.SemaphoreType.DMA((7,)),
        ],
        far=5, name="pack",
    )
    pairs = [(i, i + 1) for i in range(1, devices - 1, 2)]
    from_chip = lax.ppermute(to_chip, BLOCKS, pairs + [(j, i) for i, j in pairs])
    from_core = lax.ppermute(to_core, "core", [(0, 1), (1, 0)])
    outer, inner, bands, spread, dpre, dy, state = call(
        inner_kernel,
        [
            ((8, 80, full), BF16), ((8, 64, full), BF16), ((3, TAPS, ROW), BF16), ((ROW, 4 * ROW), BF16),
            ((6, 64, ROW), BF16), ((8, 64, ROW), F32), ((4, 128, ROW), BF16),
        ],
        [live, fine, conv, down, coarse],
        [pltpu.VMEM((384, ROW), F32), pltpu.VMEM((128, 4 * ROW), F32)],
        name="inner",
    )
    grads, dpre = call(
        lambda *refs: main_kernel(scale, *refs),
        [((GRADS, 128), SENT), ((10, 64, ROW), BF16)],
        [inner, outer, from_chip, from_core, coarse, bands, spread, dpre, dy, state],
        [
            pltpu.VMEM((12, 80, full), BF16), pltpu.VMEM((12, 64, full), BF16), pltpu.VMEM((2, 32, ROW), BF16),
            pltpu.VMEM((2, 128, ROW), F32), pltpu.VMEM((4, 128, ROW), BF16),
        ],
        name="main",
    )
    near, far = lax.axis_size(NEAR), lax.axis_size("z")
    plane = plane_order()
    add = functools.partial(sum_kernel, GRADS // near)
    parts = exchange(grads, NEAR, [plane])
    def back(turn, arrays):
        (result,) = call(
            functools.partial(back_turn, turn), [((8, 64 * ROW), BF16)], arrays + [live, conv, dpre, dy],
            [
                pltpu.VMEM((8, 64 * ROW), BF16), pltpu.VMEM((10, 80, WIDE), BF16),
                pltpu.VMEM((10, 64, WIDE), BF16), pltpu.VMEM((3, TAPS, ROW), BF16),
                pltpu.SemaphoreType.DMA((1,)),
            ],
            far=turn, out_space=pltpu.HBM, same=[(0, 0)] * turn, name=f"back{turn}",
        )
        return result

    parts, dpre = lax.optimization_barrier((parts, dpre))
    result = back(0, [])
    (sums,) = call(add, [((far * GRADS // near, 128), SENT)], [parts], name="sum_near")
    sums, result = lax.optimization_barrier((sums, result))
    sums = exchange(sums, "z", [[(k + far // 2) % far for k in range(far)]])
    (sums,) = call(add, [((GRADS, 128), SENT)], [sums], name="sum_far")
    whole, result = lax.optimization_barrier((exchange(sums, NEAR, [plane]), result))
    conv_grad, down_grad = call(
        finish_kernel, [((27, 32, 32), F32), ((8, 32, 64), F32)], [whole], name="finish"
    )
    result = back(1, [result])
    return result[None], conv_grad, down_grad


def solution(mesh):
    fine = Mesh(mesh.devices.reshape(-1, 4, 2, mesh.shape["vol"]), BLOCKS + ("vol",))
    placed = (P("vol", BLOCKS, None), P("vol", BLOCKS), P("vol", BLOCKS, None), P(), P())
    return jax.shard_map(
        shards,
        mesh=fine,
        in_specs=placed,
        out_specs=(P("vol", BLOCKS, None), P(), P()),
        check_vma=False,
    )
```
